32 devices in a mesh: groups: 2 (over y), node: 4 (over z), row: 2 (over x), sub: 2 (over core).
Axes of the slice: x: 2, y: 2, z: 4, core: 2. Of those that a mesh axis runs over, the one named last changes fastest.
Arguments:
- root_inverse: float32 [8, 256, 4, 256], P(('groups', 'node'), 'row'), parts along dimension 0
- panel_one: float32 [16, 4, 256, 256], P(('groups', 'node'), None, 'row', 'sub'), parts along dimension 0, may hold values from -0.1875 to 0.1875
- diag_one: float32 [16, 256, 256], P(('groups', 'node'), 'row', 'sub'), parts along dimension 0, may hold values from -3 to 3
- panel_two: float32 [32, 4, 256, 256], P(('groups', 'node'), None, 'row', 'sub'), parts along dimension 0, may hold values from -0.1875 to 0.1875
- diag_two: float32 [32, 256, 256], P(('groups', 'node'), 'row', 'sub'), parts along dimension 0, may hold values from -3 to 3
- ancestors: int32 [16, 4], P('groups'), parts along dimension 0, may hold values from 0 to 3, as said below
- counts: int32 [16], P('groups'), parts along dimension 0, may hold values from 1 to 4
- owners: int32 [32], P('groups'), parts along dimension 0, may hold values from 0 to 3, as said below
- slots: int32 [32], P('groups'), parts along dimension 0, may hold values from 0 to 1
- offsets: int32 [32, 3], P('groups'), parts along dimension 0, may hold values from 0 to 3, as said below
Outputs:
- cov_panel_one: float32 [16, 4, 256, 256], P(('groups', 'node'), None, 'row', 'sub'), parts along dimension 0
- cov_diag_one: float32 [16, 256, 256], P(('groups', 'node'), 'row', 'sub'), parts along dimension 0
- cov_panel_two: float32 [32, 4, 256, 256], P(('groups', 'node'), None, 'row', 'sub'), parts along dimension 0
- cov_diag_two: float32 [32, 256, 256], P(('groups', 'node'), 'row', 'sub'), parts along dimension 0
The draws below stay inside these ranges and needn't reach their ends.
There are 2 independent parts, one for each index of `groups`. The reference program is written for one: setup_inputs(seed, part) draws one part's arguments, and reference() takes and returns one part's arrays. A program takes and returns all parts, laid end to end along the dimension named above; each array names one. Nothing has to cross between parts.
Inputs may be any that keep to these rules, and one draw needn't show every extreme that they name: `ancestors`: the ids of one supernode are distinct; all 2 supernodes of one node index share their first id. `owners`: the 4 supernodes of one node index have parents on different node indices. `offsets`: distinct within a row; the first min(3, counts of the parent) entries are below that count.
All inputs are finite; a program needn't handle non-finite values.
Results may differ from the reference program's by a relative error of at most 0.0003.
Values sent between devices are 32-bit elements; how exact they have to be, the bound alone decides.
No kernel may reach another device: no remote copies, remote signals or barrier semaphores. Data moves between devices by JAX's collectives and lax.ppermute only.
A program may use at most 64 MiB of HBM per device.

```python
import jax
import jax.numpy as jnp
from jax import lax

BS = 256
A = 4
SUP1_DEV = 2
SUP2_DEV = 4
ROOTB = 4
SUP1 = 8
SUP2 = 16
N_NODE = 4


def common_tree(key):
    keys = jax.random.split(key, 9)
    hot_block = jax.random.randint(keys[0], (N_NODE,), 0, ROOTB)
    hot_rows = jnp.repeat(hot_block, SUP1_DEV)
    ranking = jax.random.permutation(keys[1], ROOTB).astype(jnp.int32)
    columns = jnp.arange(ROOTB, dtype=jnp.int32)
    scores = jax.random.randint(keys[2], (SUP1, ROOTB), 0, 4096) + ranking[None, :] * 512
    scores = scores * ROOTB + columns[None, :]
    scores = jnp.where(columns[None, :] == hot_rows[:, None], -1, scores)
    others = lax.top_k(scores, A - 1)[1].astype(jnp.int32)
    ancestors = jnp.concatenate([hot_rows[:, None].astype(jnp.int32), others], axis=1)
    node_ids = jnp.arange(N_NODE, dtype=jnp.int32)
    bias = jax.random.permutation(keys[5], N_NODE).astype(jnp.int32)
    owner_scores = jax.random.randint(keys[6], (N_NODE, N_NODE), 0, 1024) + bias[None, :] * 256
    owner_scores = owner_scores * N_NODE + node_ids[None, :]
    owners = lax.top_k(owner_scores, SUP2_DEV)[1].reshape(SUP2).astype(jnp.int32)
    slots = jax.random.randint(keys[7], (SUP2,), 0, SUP1_DEV).astype(jnp.int32)
    counts = jax.random.randint(keys[3], (SUP1,), 2, A + 1)
    entries = jnp.arange(SUP1, dtype=jnp.int32)
    first_parent = owners[0] * SUP1_DEV + slots[0]
    pick = jax.random.randint(keys[4], (), 0, SUP1 - 1)
    full_pick = (first_parent + 1 + pick) % SUP1
    counts = jnp.where(entries == first_parent, 1, counts)
    counts = jnp.where(entries == full_pick, A, counts).astype(jnp.int32)
    parent_count = jnp.take(counts, owners * SUP1_DEV + slots)
    places = jnp.arange(A, dtype=jnp.int32)
    shuffled = jax.random.randint(keys[8], (SUP2, A), 0, 1024) * A + places[None, :]
    keyed = (places[None, :] >= parent_count[:, None]).astype(jnp.int32) * (1 << 20) + shuffled
    offsets = jnp.argsort(keyed, axis=1, stable=True)[:, :A - 1].astype(jnp.int32)
    return (ancestors, counts, owners, slots, offsets)


def draw_ancestors(key, part):
    return common_tree(key)[0]


def draw_counts(key, part):
    return common_tree(key)[1]


def draw_owners(key, part):
    return common_tree(key)[2]


def draw_slots(key, part):
    return common_tree(key)[3]


def draw_offsets(key, part):
    return common_tree(key)[4]


def draw_root_inverse(key, part):
    key = jax.random.fold_in(key, 7)
    shape = (ROOTB, BS, ROOTB, BS)
    raw = jax.random.normal(key, shape, jnp.float32)
    mixed = 0.25 * (raw + jnp.transpose(raw, (2, 3, 0, 1)))
    same_block = jnp.arange(ROOTB)[:, None, None, None] == jnp.arange(ROOTB)[None, None, :, None]
    same_entry = jnp.arange(BS)[None, :, None, None] == jnp.arange(BS)[None, None, None, :]
    return mixed + 2.0 * (same_block & same_entry).astype(jnp.float32)


def levels(key, extent, pieces, low, largest):
    loudness = 1.0
    for position, shards_of in pieces:
        heights = jax.random.uniform(jax.random.fold_in(jax.random.fold_in(key, 6), position), (shards_of,), jnp.float32, low / len(pieces), largest / len(pieces))
        loudness = loudness * jnp.repeat(jnp.exp(heights), extent[position] // shards_of).reshape((-1,) + (1,) * (len(extent) - 1 - position))
    return loudness


def centred(key, extent, spread, reach, cuts=(), kind=jnp.bfloat16):
    factor_of = levels(key, extent, cuts, -0.22, 0.18) if cuts else 1.0
    array = jax.random.normal(key, extent, jnp.float32) * spread * factor_of
    return jnp.minimum(jnp.maximum(array, -reach), reach).astype(kind)


def setup_inputs(seed: int = 0, part: int = 0) -> dict:
    streams_of = jax.random.split(jax.random.key(seed), 11)
    part_splits = jax.random.split(jax.random.fold_in(streams_of[10], part), 11)
    root_inverse = draw_root_inverse(jax.random.fold_in(jax.random.fold_in(streams_of[10], part), 71), part)
    panel_one = centred(part_splits[1], (SUP1, A, BS, BS), (A * BS) ** -0.5, 0.1875, ((0, 4), (2, 2), (3, 2)), jnp.float32)
    diag_one = centred(part_splits[2], (SUP1, BS, BS), 0.5, 3.0, ((0, 4), (1, 2), (2, 2)), jnp.float32)
    panel_two = centred(part_splits[3], (SUP2, A, BS, BS), (A * BS) ** -0.5, 0.1875, ((0, 4), (2, 2), (3, 2)), jnp.float32)
    diag_two = centred(part_splits[4], (SUP2, BS, BS), 0.5, 3.0, ((0, 4), (1, 2), (2, 2)), jnp.float32)
    ancestors = draw_ancestors(jax.random.fold_in(jax.random.fold_in(streams_of[10], part), 71), part)
    counts = draw_counts(jax.random.fold_in(jax.random.fold_in(streams_of[10], part), 71), part)
    owners = draw_owners(jax.random.fold_in(jax.random.fold_in(streams_of[10], part), 71), part)
    slots = draw_slots(jax.random.fold_in(jax.random.fold_in(streams_of[10], part), 71), part)
    offsets = draw_offsets(jax.random.fold_in(jax.random.fold_in(streams_of[10], part), 71), part)
    return dict(root_inverse=root_inverse, panel_one=panel_one, diag_one=diag_one, panel_two=panel_two, diag_two=diag_two, ancestors=ancestors, counts=counts, owners=owners, slots=slots, offsets=offsets)


PRECISE = lax.Precision.HIGHEST


def reference(root_inverse, panel_one, diag_one, panel_two, diag_two, ancestors, counts, owners, slots, offsets):
    positions = jnp.arange(A, dtype=jnp.int32)

    def level_one(record):
        block_ids, live_count, factor, diagonal = record
        usable = (positions < live_count).astype(jnp.float32)
        root_rows = jnp.take(root_inverse, block_ids, axis=0)
        matrix = jnp.take(root_rows, block_ids, axis=2) * usable[:, None, None, None]
        masked = factor * usable[:, None, None]
        column = -jnp.einsum("aibc,bcj->aij", matrix, masked, precision=PRECISE)
        return column, diagonal - jnp.einsum("aij,ail->jl", masked, column, precision=PRECISE)

    cov_panel_one, cov_diag_one = lax.map(level_one, (ancestors, counts, panel_one, diag_one))

    def level_two(record):
        owner_dev, slot_pos, offsets_row, factor, diagonal = record
        parent = owner_dev * SUP1_DEV + slot_pos
        live_count = jnp.minimum(A, 1 + counts[parent])
        usable = (positions < live_count).astype(jnp.float32)
        block_ids = jnp.take(ancestors[parent], offsets_row)
        beside = jnp.take(cov_panel_one[parent], offsets_row, axis=0)
        root_rows = jnp.take(root_inverse, block_ids, axis=0)
        root_part = jnp.take(root_rows, block_ids, axis=2)
        top_row = jnp.concatenate([cov_diag_one[parent][:, None, :], jnp.transpose(beside, (2, 0, 1))], axis=1)
        lower_rows = jnp.concatenate([beside[:, :, None, :], root_part], axis=2)
        matrix = jnp.concatenate([top_row[None], lower_rows], axis=0) * usable[:, None, None, None]
        masked = factor * usable[:, None, None]
        column = -jnp.einsum("aibc,bcj->aij", matrix, masked, precision=PRECISE)
        return column, diagonal - jnp.einsum("aij,ail->jl", masked, column, precision=PRECISE)

    cov_panel_two, cov_diag_two = lax.map(level_two, (owners, slots, offsets, panel_two, diag_two))
    return (cov_panel_one, cov_diag_one, cov_panel_two, cov_diag_two)
```

```python
import functools

import jax
import jax.numpy as jnp
from jax import lax
from jax.experimental import pallas as pl
from jax.experimental.pallas import tpu as pltpu
from jax.sharding import PartitionSpec as P

A = 4


PRECISE = lax.Precision.HIGHEST
THREE_PASS = lax.Precision.HIGH
F32 = jnp.float32
SMEM = pl.BlockSpec(memory_space=pltpu.SMEM)
VMEM = pl.BlockSpec(memory_space=pltpu.VMEM)


def mm(a, b):
    return jnp.dot(a, b, precision=THREE_PASS, preferred_element_type=F32)


def mm_t(a, b):
    return lax.dot_general(
        a, b, (((0,), (0,)), ((), ())), precision=THREE_PASS, preferred_element_type=F32
    )


def call(body, out_shapes, operands, n_smem, scratch=(), aliases=None, flops=0):
    size = sum(4 * o.size for o in operands) + sum(4 * o.size for o in out_shapes)
    return pl.pallas_call(
        body,
        out_shape=tuple(out_shapes),
        in_specs=[SMEM] * n_smem + [VMEM] * (len(operands) - n_smem),
        out_specs=tuple([VMEM] * len(out_shapes)),
        scratch_shapes=list(scratch),
        input_output_aliases=aliases or {},
        compiler_params=pltpu.CompilerParams(vmem_limit_bytes=40 * 1024 * 1024),
        cost_estimate=pl.CostEstimate(flops=flops, bytes_accessed=size, transcendentals=0),
    )(*operands)


def find_child(owners, node, owner, per_two):
    found = jnp.int32(0)
    for c in range(per_two):
        found = jnp.where(owners[node * per_two + c] == owner, c, found)
    return found


def spot(index, size):
    return pl.ds(pl.multiple_of(index * size, size), size)


def level_one_kernel(nodes, place, ids, counts, owners, slots, offsets, *refs):
    shifts = nodes - 1
    root = refs[0]
    far = refs[1 : 1 + shifts]
    near = refs[1 + shifts : 1 + 2 * shifts]
    own, beside, across = refs[1 + 2 * shifts : 4 + 2 * shifts]
    outs = refs[4 + 2 * shifts :]
    whole, cov, keep, send = outs[:4]
    picks = outs[4 : 4 + nodes]
    spread, wide, tall, part = outs[4 + nodes :]
    me, row, sub = place[0], place[1], place[2]
    per_one, a_count, rows, cols = own.shape
    half = rows // 2
    width = root.shape[2]
    blocks = root.shape[1]
    for b in range(blocks):
        whole[spot(me, rows), b * width : (b + 1) * width] = root[:, b, :]
    for k in range(1, nodes):
        block = lax.rem(me - k + nodes, nodes)
        for b in range(blocks):
            lanes = slice(b * width, (b + 1) * width)
            whole[spot(block * 2 + sub, half), lanes] = far[k - 1][:, b, :]
            whole[spot(block * 2 + 1 - sub, half), lanes] = near[k - 1][:, b, :]
    for g in range(per_one):
        for a in range(a_count):
            at = ids[me * per_one + g, a]
            valid = (a < counts[me * per_one + g]).astype(F32)
            lanes = slice(g * cols, (g + 1) * cols)
            spread[spot(at * 2 + row, rows), lanes] = own[g, a] * valid
            spread[spot(at * 2 + 1 - row, rows), lanes] = beside[g, a] * valid
    total = mm(whole[...], spread[...])
    for g in range(per_one):
        tall[g] = total[:, g * cols : (g + 1) * cols]
    for g in range(per_one):
        for a in range(a_count):
            at = ids[me * per_one + g, a]
            valid = (a < counts[me * per_one + g]).astype(F32)
            cov[g, a] = tall[g, spot(at, rows), :] * (-valid)
            wide[a * rows : (a + 1) * rows, spot(sub, cols)] = own[g, a] * valid
            wide[a * rows : (a + 1) * rows, spot(1 - sub, cols)] = across[g, a] * valid
        part[...] = -mm_t(wide[...], cov[g].reshape(a_count * rows, cols))
        keep[g] = part[spot(row, rows), :]
        send[g] = part[spot(1 - row, rows), :]
    per_two = owners.shape[0] // nodes
    for k in range(nodes):
        target = lax.rem(me + k, nodes)
        child = target * per_two + find_child(owners, target, me, per_two)
        for t in range(a_count - 1):
            picks[k][t] = cov[slots[child], offsets[child, t]]


def diag_one_kernel(nodes, place, owners, slots, diagonal, keep, got, *outs):
    me = place[0]
    outs[0][...] = diagonal[...] + (keep[...] + got[...])
    per_two = owners.shape[0] // nodes
    for k in range(nodes):
        target = lax.rem(me + k, nodes)
        child = target * per_two + find_child(owners, target, me, per_two)
        outs[1 + k][...] = outs[0][slots[child]]


def parent_facts(me, h, ids, counts, owners, slots, offsets, per_one, per_two):
    child = me * per_two + h
    parent = owners[child] * per_one + slots[child]
    count = counts[parent]
    valid = [(t < 1 + count).astype(F32) for t in range(A)]
    blocks = [ids[parent, offsets[child, t]] for t in range(A - 1)]
    return valid, blocks


def root_two_kernel(per_one, place, ids, counts, owners, slots, offsets, whole, own, beside, across, lower, inner, spread, wide, tall):
    me, row, sub = place[0], place[1], place[2]
    per_two, a_count, rows, cols = own.shape
    spread[...] = jnp.zeros_like(spread)
    for h in range(per_two):
        valid, at = parent_facts(me, h, ids, counts, owners, slots, offsets, per_one, per_two)
        lanes = slice(h * cols, (h + 1) * cols)
        for t in range(1, a_count):
            spread[spot(at[t - 1] * 2 + row, rows), lanes] = own[h, t] * valid[t]
            spread[spot(at[t - 1] * 2 + 1 - row, rows), lanes] = beside[h, t] * valid[t]
    total = mm(whole[...], spread[...])
    for h in range(per_two):
        tall[h] = total[:, h * cols : (h + 1) * cols]
    for h in range(per_two):
        valid, at = parent_facts(me, h, ids, counts, owners, slots, offsets, per_one, per_two)
        for t in range(1, a_count):
            lower[h, t - 1] = tall[h, spot(at[t - 1], rows), :] * valid[t]
            wide[(t - 1) * rows : t * rows, spot(sub, cols)] = own[h, t] * valid[t]
            wide[(t - 1) * rows : t * rows, spot(1 - sub, cols)] = across[h, t] * valid[t]
        inner[h] = mm_t(wide[...], lower[h].reshape((a_count - 1) * rows, cols))


def parent_two_kernel(nodes, per_one, shifts, chained, place, ids, counts, owners, slots, offsets, own, beside, across, corner, lower, inner, diagonal, *refs):
    me, row, sub = place[0], place[1], place[2]
    per_two, a_count, rows, cols = own.shape
    refs = list(refs)
    ins = [refs[4 * i : 4 * i + 4] for i in range(len(shifts))]
    refs = refs[4 * len(shifts) :]
    if chained:
        refs = refs[2:]
    panel, diag = refs[:2]
    sends = refs[2 : 2 + len(shifts)]
    cross, top, first, local, wide, part, more = refs[2 + len(shifts) :]
    low = (a_count - 1) * rows
    for i, k in enumerate(shifts):
        cross_own, cross_side, top_own, top_side = ins[i]
        source = lax.rem(me - k + nodes, nodes)
        h = find_child(owners, me, source, per_two)
        valid, _ = parent_facts(me, h, ids, counts, owners, slots, offsets, per_one, per_two)
        for t in range(1, a_count):
            span = slice((t - 1) * rows, t * rows)
            cross[span, spot(sub, cols)] = cross_own[t - 1]
            cross[span, spot(1 - sub, cols)] = cross_side[t - 1]
            local[span, :] = own[h, t] * valid[t]
            wide[span, spot(sub, cols)] = own[h, t] * valid[t]
            wide[span, spot(1 - sub, cols)] = across[h, t] * valid[t]
        top[:, spot(sub, cols)] = top_own[...]
        top[:, spot(1 - sub, cols)] = top_side[...]
        first[spot(row, rows), :] = own[h, 0]
        first[spot(1 - row, rows), :] = beside[h, 0]
        mine, other = low + row * rows, low + (1 - row) * rows
        mine, other = pl.multiple_of(mine, rows), pl.multiple_of(other, rows)
        wide[pl.ds(mine, rows), spot(sub, cols)] = own[h, 0]
        wide[pl.ds(mine, rows), spot(1 - sub, cols)] = across[h, 0]
        wide[pl.ds(other, rows), spot(sub, cols)] = beside[h, 0]
        wide[pl.ds(other, rows), spot(1 - sub, cols)] = corner[h]
        below = mm(cross[...], first[...])
        for t in range(1, a_count):
            span = slice((t - 1) * rows, t * rows)
            part[span, :] = below[span, :] * valid[t]
            panel[h, t] = -(lower[h, t - 1] + part[span, :])
        part[low:, :] = mm_t(cross[...], local[...])
        part[pl.ds(mine, rows), :] += mm(top[...], first[...])
        more[...] = inner[h] + mm_t(wide[...], part[...])
        panel[h, 0] = -part[pl.ds(mine, rows), :]
        sends[i][0] = part[pl.ds(other, rows), :]
        diag[h] = diagonal[h] + more[spot(row, rows), :]
        sends[i][1] = more[spot(1 - row, rows), :]


def finish_kernel(nodes, place, owners, *refs):
    me = place[0]
    per_two = owners.shape[0] // nodes
    got = refs[:nodes]
    panel, diag, panel_out, diag_out = refs[nodes:]
    for k in range(nodes):
        h = find_child(owners, me, lax.rem(me - k + nodes, nodes), per_two)
        panel_out[h, 0] = panel[h, 0] - got[k][0]
        diag_out[h] = diag[h] + got[k][1]


def shift(x, axis, k):
    n = lax.axis_size(axis)
    return lax.ppermute(x, axis, [(i, (i + k) % n) for i in range(n)])


def paired_shards(root_inverse, panel_one, diag_one, panel_two, diag_two, ancestors, counts, owners, slots, offsets):
    nodes = lax.axis_size("node")
    me, row, sub = lax.axis_index("node"), lax.axis_index("row"), lax.axis_index("sub")
    place = jnp.stack([me, row, sub]).astype(jnp.int32)
    per_one, a_count, rows, cols = panel_one.shape
    per_two = panel_two.shape[0]
    width = root_inverse.shape[3]
    full = root_inverse.shape[2] * width
    root = root_inverse[0]
    half = lax.dynamic_slice_in_dim(root, sub * (rows // 2), rows // 2, 0)
    far = [shift(half, "node", k) for k in range(1, nodes)]
    near = [shift(x, "sub", 1) for x in far]
    beside_one = shift(panel_one, "row", 1)
    across_one = shift(panel_one, "sub", 1)
    beside_two = shift(panel_two, "row", 1)
    across_two = shift(panel_two, "sub", 1)
    corner_two = shift(beside_two[:, 0], "sub", 1)
    S = lambda *shape: jax.ShapeDtypeStruct(shape, F32)
    tables = [place, ancestors, counts, owners, slots, offsets]

    out = call(
        functools.partial(level_one_kernel, nodes),
        [S(rows * nodes, full), S(*panel_one.shape), S(per_one, rows, cols), S(per_one, rows, cols)]
        + [S(a_count - 1, rows, cols)] * nodes,
        tables + [root] + far + near + [panel_one, beside_one, across_one],
        len(tables),
        [
            pltpu.VMEM((full, per_one * cols), F32),
            pltpu.VMEM((a_count * rows, 2 * cols), F32),
            pltpu.VMEM((per_one, rows * nodes, cols), F32),
            pltpu.VMEM((2 * rows, cols), F32),
        ],
        flops=6 * rows * nodes * full * per_one * cols,
    )
    whole, cov_panel_one, keep, send = out[:4]
    picks = out[4:]
    got_cross = [picks[0]] + [shift(picks[k], "node", k) for k in range(1, nodes)]
    cross_side = [shift(x, "sub", 1) for x in got_cross]
    got_diag = shift(send, "row", 1)
    out = call(
        functools.partial(diag_one_kernel, nodes),
        [S(*diag_one.shape)] + [S(rows, cols)] * nodes,
        [place, owners, slots, diag_one, keep, got_diag],
        3,
    )
    cov_diag_one = out[0]
    got_top = [out[1]] + [shift(out[1 + k], "node", k) for k in range(1, nodes)]
    top_side = [shift(x, "sub", 1) for x in got_top]

    lower, inner = call(
        functools.partial(root_two_kernel, per_one),
        [S(per_two, a_count - 1, rows, cols), S(per_two, 2 * rows, cols)],
        tables + [whole, panel_two, beside_two, across_two],
        len(tables),
        [
            pltpu.VMEM((full, per_two * cols), F32),
            pltpu.VMEM(((a_count - 1) * rows, 2 * cols), F32),
            pltpu.VMEM((per_two, rows * nodes, cols), F32),
        ],
        flops=6 * rows * nodes * full * per_two * cols,
    )

    low = (a_count - 1) * rows
    groups = [tuple(range(nodes))]
    sends = {}
    state = ()
    for ks in groups:
        arrived = []
        for k in ks:
            arrived += [got_cross[k], cross_side[k], got_top[k], top_side[k]]
        operands = (
            tables
            + [panel_two, beside_two, across_two, corner_two, lower, inner, diag_two]
            + arrived
            + list(state)
        )
        n = len(operands)
        out = call(
            functools.partial(parent_two_kernel, nodes, per_one, ks, bool(state)),
            [S(*panel_two.shape), S(*diag_two.shape)] + [S(2, rows, cols)] * len(ks),
            operands,
            len(tables),
            [
                pltpu.VMEM((low, 2 * cols), F32),
                pltpu.VMEM((rows, 2 * cols), F32),
                pltpu.VMEM((2 * rows, cols), F32),
                pltpu.VMEM((low, cols), F32),
                pltpu.VMEM((low + 2 * rows, 2 * cols), F32),
                pltpu.VMEM((low + 2 * rows, cols), F32),
                pltpu.VMEM((2 * rows, cols), F32),
            ],
            aliases={n - 2: 0, n - 1: 1} if state else None,
            flops=6 * len(ks) * 6 * low * cols * 2 * cols,
        )
        state = out[:2]
        for k, x in zip(ks, out[2:]):
            sends[k] = x
    got = [shift(sends[k], "row", 1) for k in range(nodes)]
    cov_panel_two, cov_diag_two = finish(nodes, place, owners, got, *state)
    return (cov_panel_one, cov_diag_one, cov_panel_two, cov_diag_two)


def finish(nodes, place, owners, got, panel, diag):
    per_two, _, rows, cols = panel.shape
    firsts = pl.BlockSpec((per_two, 1, rows, cols), lambda i: (0, 0, 0, 0))
    whole = pl.BlockSpec(diag.shape, lambda i: (0, 0, 0))
    n = 2 + nodes
    return pl.pallas_call(
        functools.partial(finish_kernel, nodes),
        grid=(1,),
        out_shape=(
            jax.ShapeDtypeStruct(panel.shape, F32),
            jax.ShapeDtypeStruct(diag.shape, F32),
        ),
        in_specs=[SMEM] * 2 + [VMEM] * nodes + [firsts, whole],
        out_specs=(firsts, whole),
        input_output_aliases={n: 0, n + 1: 1},
        compiler_params=pltpu.CompilerParams(vmem_limit_bytes=16 * 1024 * 1024),
        cost_estimate=pl.CostEstimate(flops=0, bytes_accessed=3 * 8 * diag.size, transcendentals=0),
    )(place, owners, *got, panel, diag)


def pick_blocks(gathered, block_ids):
    return gathered[block_ids[:, :, None], :, block_ids[:, None, :]]


def apply_panel(matrix, masked):
    return jnp.einsum(
        "kabic,kbcj->kaij",
        matrix,
        lax.all_gather(masked, "row", axis=2, tiled=True),
        precision=PRECISE,
    )


def diag_update(masked, column, diagonal):
    full_cols = lax.all_gather(masked, "sub", axis=3, tiled=True)
    summed = lax.psum_scatter(
        jnp.einsum("kaij,kail->jkl", full_cols, column, precision=PRECISE),
        "row",
        scatter_dimension=0,
        tiled=True,
    )
    return diagonal - jnp.transpose(summed, (1, 0, 2))


def general_shards(
    root_inverse,
    panel_one,
    diag_one,
    panel_two,
    diag_two,
    ancestors,
    counts,
    owners,
    slots,
    offsets,
):
    nodes = lax.axis_size("node")
    own_index = lax.axis_index("node")
    per_one = panel_one.shape[0]
    per_two = panel_two.shape[0]
    rows_here = panel_one.shape[2]
    width = root_inverse.shape[3]
    positions = jnp.arange(A, dtype=jnp.int32)
    my_ids = lax.dynamic_slice_in_dim(ancestors, own_index * per_one, per_one, 0)
    my_counts = lax.dynamic_slice_in_dim(counts, own_index * per_one, per_one, 0)
    valid_one = (positions[None, :] < my_counts[:, None]).astype(jnp.float32)
    my_owner = lax.dynamic_slice_in_dim(owners, own_index * per_two, per_two, 0)
    my_slot = lax.dynamic_slice_in_dim(slots, own_index * per_two, per_two, 0)
    my_offsets = lax.dynamic_slice_in_dim(offsets, own_index * per_two, per_two, 0)
    my_parent = my_owner * per_one + my_slot
    parent_count = jnp.take(counts, my_parent)
    valid_two = (positions[None, :] < jnp.minimum(A, 1 + parent_count)[:, None]).astype(jnp.float32)
    gathered = lax.all_gather(root_inverse, "node", axis=0, tiled=True)
    block_one = pick_blocks(gathered, my_ids)
    parent_ids = jnp.take_along_axis(jnp.take(ancestors, my_parent, axis=0), my_offsets, axis=1)
    separator = pick_blocks(gathered, parent_ids)
    block_one = block_one * valid_one[:, :, None, None, None]
    masked_one = panel_one * valid_one[:, :, None, None]
    cov_panel_one = -apply_panel(block_one, masked_one)
    cov_diag_one = diag_update(masked_one, cov_panel_one, diag_one)
    full_cross, full_diag = (
        lax.all_gather(cov_panel_one, "sub", axis=3, tiled=True),
        lax.all_gather(cov_diag_one, "sub", axis=2, tiled=True),
    )
    owner_grid = owners.reshape(nodes, per_two)
    child_match = (owner_grid == own_index).astype(jnp.int32)
    has_child = jnp.sum(child_match, axis=1)
    child_pos = jnp.sum(child_match * jnp.arange(per_two, dtype=jnp.int32)[None, :], axis=1)
    child_index = jnp.arange(nodes, dtype=jnp.int32) * per_two + child_pos
    parent_slot = jnp.take(slots, child_index)
    parent_pos = jnp.take(offsets, child_index, axis=0)
    present = has_child.astype(jnp.float32)
    top_send = jnp.take(full_diag, parent_slot, axis=0) * present[:, None, None]
    cross_pick = jnp.take(
        full_cross.reshape(per_one * A, rows_here, width),
        parent_slot[:, None] * A + parent_pos,
        axis=0,
    )
    cross_pick = cross_pick * present[:, None, None, None]
    got_top, got_cross = (
        lax.all_to_all(top_send, "node", split_axis=0, concat_axis=0, tiled=True),
        lax.all_to_all(cross_pick, "node", split_axis=0, concat_axis=0, tiled=True),
    )
    my_cross = jnp.take(got_cross, my_owner, axis=0)
    my_lower = jnp.concatenate([my_cross[:, :, None], separator], axis=2)
    my_top = jnp.take(got_top, my_owner, axis=0)
    empty_blocks = jnp.zeros((per_two, 1, A - 1, rows_here, width), jnp.float32)
    first_row = jnp.concatenate([my_top[:, None, None], empty_blocks], axis=2)
    block_two = jnp.concatenate([first_row, my_lower], axis=1) * valid_two[:, :, None, None, None]
    masked_two = panel_two * valid_two[:, :, None, None]
    lower_part = apply_panel(block_two, masked_two)
    beside = my_lower[:, :, 0]
    further = masked_two[:, 1:]
    upper_part = lax.psum_scatter(
        jnp.einsum("ktci,ktcj->ikj", beside, further, precision=PRECISE),
        "row",
        scatter_dimension=0,
        tiled=True,
    )
    first_block = lower_part[:, 0] + jnp.transpose(upper_part, (1, 0, 2))
    cov_panel_two = -jnp.concatenate([first_block[:, None], lower_part[:, 1:]], axis=1)
    cov_diag_two = diag_update(masked_two, cov_panel_two, diag_two)
    return (cov_panel_one, cov_diag_one, cov_panel_two, cov_diag_two)


def shards(*args):
    sizes = lax.axis_size("node"), lax.axis_size("row"), lax.axis_size("sub")
    root, panel_one, panel_two = args[0], args[1], args[3]
    if panel_two.shape[0] == sizes[0] == root.shape[2] and sizes[1:] == (2, 2) and root.shape[0] == 1 and panel_one.shape[1] == A:
        return paired_shards(*args)
    return general_shards(*args)


def solution(mesh):
    return jax.shard_map(
        shards,
        mesh=mesh,
        in_specs=(
            P(("groups", "node"), "row", None, None),
            P(("groups", "node"), None, "row", "sub"),
            P(("groups", "node"), "row", "sub"),
            P(("groups", "node"), None, "row", "sub"),
            P(("groups", "node"), "row", "sub"),
            P("groups", None),
            P("groups"),
            P("groups"),
            P("groups"),
            P("groups", None),
        ),
        out_specs=(
            P(("groups", "node"), None, "row", "sub"),
            P(("groups", "node"), "row", "sub"),
            P(("groups", "node"), None, "row", "sub"),
            P(("groups", "node"), "row", "sub"),
        ),
        check_vma=False,
    )
```

```python
import functools

import jax
import jax.numpy as jnp
from jax import lax
from jax.experimental import pallas as pl
from jax.experimental.pallas import tpu as pltpu
from jax.sharding import PartitionSpec as P

A = 4


PRECISE = lax.Precision.HIGHEST
THREE_PASS = lax.Precision.HIGH
F32 = jnp.float32
SMEM = pl.BlockSpec(memory_space=pltpu.SMEM)
VMEM = pl.BlockSpec(memory_space=pltpu.VMEM)


def mm(a, b):
    return jnp.dot(a, b, precision=THREE_PASS, preferred_element_type=F32)


def mm_t(a, b):
    return lax.dot_general(
        a, b, (((0,), (0,)), ((), ())), precision=THREE_PASS, preferred_element_type=F32
    )


def array(*shape):
    return jax.ShapeDtypeStruct(shape, F32)


def call(body, out_shapes, table, operands, scratch=(), flops=0):
    size = sum(4 * o.size for o in operands) + sum(4 * o.size for o in out_shapes)
    return pl.pallas_call(
        body,
        out_shape=tuple(out_shapes),
        in_specs=[SMEM] + [VMEM] * len(operands),
        out_specs=tuple([VMEM] * len(out_shapes)),
        scratch_shapes=[pltpu.VMEM(s, F32) for s in scratch],
        compiler_params=pltpu.CompilerParams(vmem_limit_bytes=40 * 1024 * 1024),
        cost_estimate=pl.CostEstimate(flops=0, bytes_accessed=0, transcendentals=0),
    )(table, *operands)


def spot(index, size):
    return pl.ds(pl.multiple_of(index * size, size), size)


class Tree:
    def __init__(self, table, nodes, per_one, per_two):
        self.table, self.nodes, self.per_one, self.per_two = table, nodes, per_one, per_two
        self.ones, self.twos = nodes * per_one, nodes * per_two
        self.me, self.row, self.sub = table[0], table[1], table[2]

    def count(self, g):
        return self.table[3 + g]

    def owner(self, h):
        return self.table[3 + self.ones + h]

    def slot(self, h):
        return self.table[3 + self.ones + self.twos + h]

    def ancestor(self, g, a):
        return self.table[3 + self.ones + 2 * self.twos + a * self.ones + g]

    def offset(self, h, t):
        return self.table[3 + (1 + A) * self.ones + (2 + t) * self.twos + h]

    def node(self, k):
        return lax.rem(self.me + k + self.nodes, self.nodes)

    def child(self, node, owner):
        found = jnp.int32(0)
        for c in range(self.per_two):
            found = jnp.where(self.owner(node * self.per_two + c) == owner, c, found)
        return found

    def back(self, block):
        return lax.rem(self.me - block + self.nodes, self.nodes)

    def live(self, g, a):
        return (a < self.count(g)).astype(F32)

    def level_two(self, h):
        h = self.me * self.per_two + h
        parent = self.owner(h) * self.per_one + self.slot(h)
        valid = [(t < 1 + self.count(parent)).astype(F32) for t in range(A)]
        return valid, [self.ancestor(parent, self.offset(h, t)) for t in range(A - 1)]


def fill_rows(out, at, rows, parts):
    for first, part in parts:
        width = part.shape[2]
        for b in range(part.shape[1]):
            out[pl.ds(pl.multiple_of(at + first, rows // 2), part.shape[0]), b * width : (b + 1) * width] = part[:, b, :]


EARLY, LATE = (1, 3), 2


def early_kernel(sizes, table, root, *refs):
    tree = Tree(table, *sizes)
    n = len(EARLY)
    far, near = refs[:n], refs[n : 2 * n]
    own, beside, whole, spread, total = refs[2 * n :]
    beside = beside.at[1 - tree.row]
    per_one, blocks, rows, cols = own.shape
    half = rows // 2
    fill_rows(whole, 0, rows, [(0, root)])
    for i in range(n):
        fill_rows(whole, (i + 1) * rows, rows, [(tree.sub * half, far[i]), ((1 - tree.sub) * half, near[i])])
    for g in range(per_one):
        for a in range(blocks):
            one = tree.me * per_one + g
            at, valid = tree.ancestor(one, a), tree.live(one, a)
            lanes = slice(g * cols, (g + 1) * cols)
            spread[spot(at * 2 + tree.row, rows), lanes] = own[g, a] * valid
            spread[spot(at * 2 + 1 - tree.row, rows), lanes] = beside[g, a] * valid
    total[...] = mm(whole[...], spread[...])


def late_kernel(sizes, table, far, near, spread, total, own, across, rest, cov, keep, send, *refs):
    tree = Tree(table, *sizes)
    picks = refs[: tree.nodes]
    wide, tall, part = refs[tree.nodes :]
    per_one, blocks, rows, cols = own.shape
    half = rows // 2
    fill_rows(rest, 0, rows, [(tree.sub * half, far), ((1 - tree.sub) * half, near)])
    last = mm(rest[...], spread[...])
    for g in range(per_one):
        lanes = slice(g * cols, (g + 1) * cols)
        for i, k in enumerate((0,) + EARLY):
            tall[g, k] = total[i * rows : (i + 1) * rows, lanes]
        tall[g, LATE] = last[:, lanes]
    for g in range(per_one):
        one = tree.me * per_one + g
        for a in range(blocks):
            cov[g, a] = tall[g, tree.back(tree.ancestor(one, a))] * (-tree.live(one, a))
    for k in range(tree.nodes):
        target = tree.node(k)
        h = target * tree.per_two + tree.child(target, tree.me)
        for t in range(blocks - 1):
            picks[k][t] = cov[tree.slot(h), tree.offset(h, t)]
    for g in range(per_one):
        one = tree.me * per_one + g
        for a in range(blocks):
            valid = tree.live(one, a)
            wide[a * rows : (a + 1) * rows, spot(tree.sub, cols)] = own[g, a] * valid
            wide[a * rows : (a + 1) * rows, spot(1 - tree.sub, cols)] = across[g, a] * valid
        part[...] = -mm_t(wide[...], cov[g].reshape(blocks * rows, cols))
        keep[g] = part[spot(tree.row, rows), :]
        send[g] = part[spot(1 - tree.row, rows), :]


def diag_one_kernel(sizes, table, diagonal, keep, got, cross, out, *tops):
    tree = Tree(table, *sizes)
    out[...] = diagonal[...] + (keep[...] + got[...])
    for k in range(tree.nodes):
        target = tree.node(k)
        slot = tree.slot(target * tree.per_two + tree.child(target, tree.me))
        if k == LATE:
            tops[k][: A - 1] = cross[...]
            tops[k][A - 1] = out[slot]
        else:
            tops[k][...] = out[slot]


def first_blocks_kernel(sizes, table, panel, out):
    tree = Tree(table, *sizes)
    out[...] = panel[1 - tree.row, :, 0]


def root_two_kernel(sizes, table, whole, rest, own, beside, across, lower, inner, spread, wide, tall):
    tree = Tree(table, *sizes)
    per_two, blocks, rows, cols = own.shape
    beside = beside.at[1 - tree.row]
    spread[...] = jnp.zeros_like(spread)
    for h in range(per_two):
        valid, at = tree.level_two(h)
        lanes = slice(h * cols, (h + 1) * cols)
        for t in range(1, blocks):
            spread[spot(at[t - 1] * 2 + tree.row, rows), lanes] = own[h, t] * valid[t]
            spread[spot(at[t - 1] * 2 + 1 - tree.row, rows), lanes] = beside[h, t] * valid[t]
    most = mm(whole[...], spread[...])
    last = mm(rest[...], spread[...])
    for h in range(per_two):
        lanes = slice(h * cols, (h + 1) * cols)
        for i, k in enumerate((0,) + EARLY):
            tall[h, k] = most[i * rows : (i + 1) * rows, lanes]
        tall[h, LATE] = last[:, lanes]
    for h in range(per_two):
        valid, at = tree.level_two(h)
        for t in range(1, blocks):
            lower[h, t - 1] = tall[h, tree.back(at[t - 1])] * valid[t]
            wide[(t - 1) * rows : t * rows, spot(tree.sub, cols)] = own[h, t] * valid[t]
            wide[(t - 1) * rows : t * rows, spot(1 - tree.sub, cols)] = across[h, t] * valid[t]
        inner[h] = mm_t(wide[...], lower[h].reshape((blocks - 1) * rows, cols))


def parent_two_kernel(sizes, shifts, table, own, beside, across, corner, lower, inner, diagonal, *refs):
    tree = Tree(table, *sizes)
    row, sub = tree.row, tree.sub
    blocks, rows, cols = own.shape[1:]
    beside = beside.at[1 - row]
    refs = list(refs)
    ins = []
    for k in shifts:
        if k == LATE:
            mine, side = refs[:2]
            del refs[:2]
            ins.append((mine, side, mine.at[A - 1], side.at[A - 1]))
        else:
            ins.append(refs[:4])
            del refs[:4]
    panel, diag, sends, cross, top, first, local, wide, part, more = refs
    low = (blocks - 1) * rows
    for i, k in enumerate(shifts):
        cross_own, cross_side, top_own, top_side = ins[i]
        h = tree.child(tree.me, tree.node(-k))
        valid, _ = tree.level_two(h)
        for t in range(1, blocks):
            span = slice((t - 1) * rows, t * rows)
            cross[span, spot(sub, cols)] = cross_own[t - 1]
            cross[span, spot(1 - sub, cols)] = cross_side[t - 1]
            local[span, :] = own[h, t] * valid[t]
            wide[span, spot(sub, cols)] = own[h, t] * valid[t]
            wide[span, spot(1 - sub, cols)] = across[h, t] * valid[t]
        top[:, spot(sub, cols)] = top_own[...]
        top[:, spot(1 - sub, cols)] = top_side[...]
        first[spot(row, rows), :] = own[h, 0]
        first[spot(1 - row, rows), :] = beside[h, 0]
        mine = spot(blocks - 1 + row, rows)
        other = spot(blocks - row, rows)
        wide[mine, spot(sub, cols)] = own[h, 0]
        wide[mine, spot(1 - sub, cols)] = across[h, 0]
        wide[other, spot(sub, cols)] = beside[h, 0]
        wide[other, spot(1 - sub, cols)] = corner[h]
        below = mm(cross[...], first[...])
        for t in range(1, blocks):
            span = slice((t - 1) * rows, t * rows)
            part[span, :] = below[span, :] * valid[t]
            panel[i, t] = -(lower[h, t - 1] + part[span, :])
        part[low:, :] = mm_t(cross[...], local[...])
        part[mine, :] += mm(top[...], first[...])
        more[...] = inner[h] + mm_t(wide[...], part[...])
        panel[i, 0] = -part[mine, :]
        sends[i, 0] = part[other, :]
        diag[i] = diagonal[h] + more[spot(row, rows), :]
        sends[i, 1] = more[spot(1 - row, rows), :]


def finish_kernel(sizes, groups, table, *refs):
    tree = Tree(table, *sizes)
    n = len(groups)
    panels, diags, gots = refs[:n], refs[n : 2 * n], refs[2 * n : 3 * n]
    panel_out, diag_out = refs[3 * n :]
    for j, shifts in enumerate(groups):
        for i, k in enumerate(shifts):
            h = tree.child(tree.me, tree.node(-k))
            panel_out[h, 1:] = panels[j][i, 1:]
            panel_out[h, 0] = panels[j][i, 0] - gots[j][i, 0]
            diag_out[h] = diags[j][i] + gots[j][i, 1]


def shift(x, axis, k):
    n = lax.axis_size(axis)
    return lax.ppermute(x, axis, [(i, (i + k) % n) for i in range(n)])


def after(x, *others):
    return lax.optimization_barrier((x,) + others)[0]


def paired_shards(root_inverse, panel_one, diag_one, panel_two, diag_two, ancestors, counts, owners, slots, offsets):
    nodes = lax.axis_size("node")
    me, row, sub = lax.axis_index("node"), lax.axis_index("row"), lax.axis_index("sub")
    per_one, blocks, rows, cols = panel_one.shape
    per_two = panel_two.shape[0]
    sizes = nodes, per_one, per_two
    full = root_inverse.shape[2] * root_inverse.shape[3]
    low = (blocks - 1) * rows
    table = jnp.concatenate(
        [jnp.stack([me, row, sub]).astype(jnp.int32), counts, owners, slots, ancestors.T.reshape(-1), offsets.T.reshape(-1)]
    )
    bind = lambda kernel, *more: functools.partial(kernel, sizes, *more)

    root = root_inverse[0]
    half = lax.dynamic_slice_in_dim(root, sub * (rows // 2), rows // 2, 0)
    far = {k: shift(half, "node", k) for k in EARLY + (LATE,)}
    beside_one = lax.all_gather(panel_one, "row")
    beside_two = lax.all_gather(panel_two, "row")
    across_one = shift(after(panel_one, *[far[k] for k in EARLY]), "sub", 1)
    across_two = shift(after(panel_two, *[far[k] for k in EARLY]), "sub", 1)
    near = {k: shift(far[k], "sub", 1) for k in EARLY}
    near[LATE] = shift(after(far[LATE], across_two), "sub", 1)

    n = len(EARLY) + 1
    whole, spread, total = call(
        bind(early_kernel),
        [array(n * rows, full), array(full, per_one * cols), array(n * rows, per_one * cols)],
        table,
        [root] + [far[k] for k in EARLY] + [near[k] for k in EARLY] + [panel_one, beside_one],
        flops=6 * n * rows * full * per_one * cols,
    )
    out = call(
        bind(late_kernel),
        [array(rows, full), array(*panel_one.shape), array(per_one, rows, cols), array(per_one, rows, cols)]
        + [array(blocks - 1, rows, cols)] * nodes,
        table,
        [far[LATE], near[LATE], spread, total, panel_one, across_one],
        [(blocks * rows, 2 * cols), (per_one, nodes, rows, cols), (2 * rows, cols)],
        flops=6 * rows * full * per_one * cols,
    )
    rest, cov_panel_one, keep, send = out[:4]
    picks = out[4:]
    cross = {k: shift(picks[k], "node", k) for k in EARLY}
    out = call(
        bind(diag_one_kernel),
        [array(*diag_one.shape)] + [array(blocks, rows, cols) if k == LATE else array(rows, cols) for k in range(nodes)],
        table,
        [diag_one, keep, shift(send, "row", 1), picks[LATE]],
    )
    cov_diag_one = out[0]
    arrived = {k: [cross[k], shift(out[1 + k], "node", k)] for k in EARLY}
    arrived[0] = [after(x, cross[EARLY[0]]) for x in (picks[0], out[1])]
    arrived[LATE] = [shift(out[1 + LATE], "node", LATE)]

    corner_two = shift(call(bind(first_blocks_kernel), [array(per_two, rows, cols)], table, [after(beside_two, cross[EARLY[0]])])[0], "sub", 1)
    lower, inner = call(
        bind(root_two_kernel),
        [array(per_two, blocks - 1, rows, cols), array(per_two, 2 * rows, cols)],
        table,
        [whole, rest, panel_two, beside_two, across_two],
        [(full, per_two * cols), (low, 2 * cols), (per_two, nodes, rows, cols)],
        flops=6 * rows * nodes * full * per_two * cols,
    )
    groups = ((0,) + EARLY, (LATE,))
    panels, diags, gots = [], [], []
    for shifts in groups:
        extra = []
        for k in shifts:
            for x in arrived[k]:
                if gots:
                    x = after(x, sends)
                extra += [x, shift(x, "sub", 1)]
        panel, diag, sends = call(
            bind(parent_two_kernel, shifts),
            [array(len(shifts), blocks, rows, cols), array(len(shifts), rows, cols), array(len(shifts), 2, rows, cols)],
            table,
            [panel_two, beside_two, across_two, corner_two, lower, inner, diag_two]
            + extra,
            [
                (low, 2 * cols),
                (rows, 2 * cols),
                (2 * rows, cols),
                (low, cols),
                (low + 2 * rows, 2 * cols),
                (low + 2 * rows, cols),
                (2 * rows, cols),
            ],
            flops=len(shifts) * 36 * low * cols * 2 * cols,
        )
        panels.append(panel)
        diags.append(diag)
        gots.append(shift(sends, "row", 1))
    cov_panel_two, cov_diag_two = call(
        bind(finish_kernel, groups),
        [array(*panel_two.shape), array(*diag_two.shape)],
        table,
        panels + diags + gots,
    )
    return (cov_panel_one, cov_diag_one, cov_panel_two, cov_diag_two)


def pick_blocks(gathered, block_ids):
    return gathered[block_ids[:, :, None], :, block_ids[:, None, :]]


def apply_panel(matrix, masked):
    return jnp.einsum(
        "kabic,kbcj->kaij",
        matrix,
        lax.all_gather(masked, "row", axis=2, tiled=True),
        precision=PRECISE,
    )


def diag_update(masked, column, diagonal):
    full_cols = lax.all_gather(masked, "sub", axis=3, tiled=True)
    summed = lax.psum_scatter(
        jnp.einsum("kaij,kail->jkl", full_cols, column, precision=PRECISE),
        "row",
        scatter_dimension=0,
        tiled=True,
    )
    return diagonal - jnp.transpose(summed, (1, 0, 2))


def general_shards(
    root_inverse,
    panel_one,
    diag_one,
    panel_two,
    diag_two,
    ancestors,
    counts,
    owners,
    slots,
    offsets,
):
    nodes = lax.axis_size("node")
    own_index = lax.axis_index("node")
    per_one = panel_one.shape[0]
    per_two = panel_two.shape[0]
    rows_here = panel_one.shape[2]
    width = root_inverse.shape[3]
    positions = jnp.arange(A, dtype=jnp.int32)
    my_ids = lax.dynamic_slice_in_dim(ancestors, own_index * per_one, per_one, 0)
    my_counts = lax.dynamic_slice_in_dim(counts, own_index * per_one, per_one, 0)
    valid_one = (positions[None, :] < my_counts[:, None]).astype(jnp.float32)
    my_owner = lax.dynamic_slice_in_dim(owners, own_index * per_two, per_two, 0)
    my_slot = lax.dynamic_slice_in_dim(slots, own_index * per_two, per_two, 0)
    my_offsets = lax.dynamic_slice_in_dim(offsets, own_index * per_two, per_two, 0)
    my_parent = my_owner * per_one + my_slot
    parent_count = jnp.take(counts, my_parent)
    valid_two = (positions[None, :] < jnp.minimum(A, 1 + parent_count)[:, None]).astype(jnp.float32)
    gathered = lax.all_gather(root_inverse, "node", axis=0, tiled=True)
    block_one = pick_blocks(gathered, my_ids)
    parent_ids = jnp.take_along_axis(jnp.take(ancestors, my_parent, axis=0), my_offsets, axis=1)
    separator = pick_blocks(gathered, parent_ids)
    block_one = block_one * valid_one[:, :, None, None, None]
    masked_one = panel_one * valid_one[:, :, None, None]
    cov_panel_one = -apply_panel(block_one, masked_one)
    cov_diag_one = diag_update(masked_one, cov_panel_one, diag_one)
    full_cross, full_diag = (
        lax.all_gather(cov_panel_one, "sub", axis=3, tiled=True),
        lax.all_gather(cov_diag_one, "sub", axis=2, tiled=True),
    )
    owner_grid = owners.reshape(nodes, per_two)
    child_match = (owner_grid == own_index).astype(jnp.int32)
    has_child = jnp.sum(child_match, axis=1)
    child_pos = jnp.sum(child_match * jnp.arange(per_two, dtype=jnp.int32)[None, :], axis=1)
    child_index = jnp.arange(nodes, dtype=jnp.int32) * per_two + child_pos
    parent_slot = jnp.take(slots, child_index)
    parent_pos = jnp.take(offsets, child_index, axis=0)
    present = has_child.astype(jnp.float32)
    top_send = jnp.take(full_diag, parent_slot, axis=0) * present[:, None, None]
    cross_pick = jnp.take(
        full_cross.reshape(per_one * A, rows_here, width),
        parent_slot[:, None] * A + parent_pos,
        axis=0,
    )
    cross_pick = cross_pick * present[:, None, None, None]
    got_top, got_cross = (
        lax.all_to_all(top_send, "node", split_axis=0, concat_axis=0, tiled=True),
        lax.all_to_all(cross_pick, "node", split_axis=0, concat_axis=0, tiled=True),
    )
    my_cross = jnp.take(got_cross, my_owner, axis=0)
    my_lower = jnp.concatenate([my_cross[:, :, None], separator], axis=2)
    my_top = jnp.take(got_top, my_owner, axis=0)
    empty_blocks = jnp.zeros((per_two, 1, A - 1, rows_here, width), jnp.float32)
    first_row = jnp.concatenate([my_top[:, None, None], empty_blocks], axis=2)
    block_two = jnp.concatenate([first_row, my_lower], axis=1) * valid_two[:, :, None, None, None]
    masked_two = panel_two * valid_two[:, :, None, None]
    lower_part = apply_panel(block_two, masked_two)
    beside = my_lower[:, :, 0]
    further = masked_two[:, 1:]
    upper_part = lax.psum_scatter(
        jnp.einsum("ktci,ktcj->ikj", beside, further, precision=PRECISE),
        "row",
        scatter_dimension=0,
        tiled=True,
    )
    first_block = lower_part[:, 0] + jnp.transpose(upper_part, (1, 0, 2))
    cov_panel_two = -jnp.concatenate([first_block[:, None], lower_part[:, 1:]], axis=1)
    cov_diag_two = diag_update(masked_two, cov_panel_two, diag_two)
    return (cov_panel_one, cov_diag_one, cov_panel_two, cov_diag_two)


def shards(*args):
    sizes = lax.axis_size("node"), lax.axis_size("row"), lax.axis_size("sub")
    root, panel_one, panel_two = args[0], args[1], args[3]
    if sizes == (4, 2, 2) and panel_two.shape[0] == root.shape[2] == panel_one.shape[1] == A and root.shape[0] == 1:
        return paired_shards(*args)
    return general_shards(*args)


def solution(mesh):
    return jax.shard_map(
        shards,
        mesh=mesh,
        in_specs=(
            P(("groups", "node"), "row", None, None),
            P(("groups", "node"), None, "row", "sub"),
            P(("groups", "node"), "row", "sub"),
            P(("groups", "node"), None, "row", "sub"),
            P(("groups", "node"), "row", "sub"),
            P("groups", None),
            P("groups"),
            P("groups"),
            P("groups"),
            P("groups", None),
        ),
        out_specs=(
            P(("groups", "node"), None, "row", "sub"),
            P(("groups", "node"), "row", "sub"),
            P(("groups", "node"), None, "row", "sub"),
            P(("groups", "node"), "row", "sub"),
        ),
        check_vma=False,
    )
```

```python
import functools

import jax
import jax.numpy as jnp
from jax import lax
from jax.experimental import pallas as pl
from jax.experimental.pallas import tpu as pltpu
from jax.sharding import PartitionSpec as P

A = 4


PRECISE = lax.Precision.HIGHEST
THREE_PASS = lax.Precision.HIGH
F32 = jnp.float32
SMEM = pl.BlockSpec(memory_space=pltpu.SMEM)
VMEM = pl.BlockSpec(memory_space=pltpu.VMEM)


def mm(a, b):
    return jnp.dot(a, b, precision=THREE_PASS, preferred_element_type=F32)


def mm_t(a, b):
    return lax.dot_general(
        a, b, (((0,), (0,)), ((), ())), precision=THREE_PASS, preferred_element_type=F32
    )


def array(*shape):
    return jax.ShapeDtypeStruct(shape, F32)


def call(body, out_shapes, table, operands, scratch=(), flops=0):
    size = sum(4 * o.size for o in operands) + sum(4 * o.size for o in out_shapes)
    return pl.pallas_call(
        body,
        out_shape=tuple(out_shapes),
        in_specs=[SMEM] + [VMEM] * len(operands),
        out_specs=tuple([VMEM] * len(out_shapes)),
        scratch_shapes=[pltpu.VMEM(s, F32) for s in scratch],
        compiler_params=pltpu.CompilerParams(vmem_limit_bytes=40 * 1024 * 1024),
        cost_estimate=pl.CostEstimate(flops=flops, bytes_accessed=0, transcendentals=0),
    )(table, *operands)


def spot(index, size):
    return pl.ds(pl.multiple_of(index * size, size), size)


class Tree:
    def __init__(self, table, nodes, per_one, per_two):
        self.table, self.nodes, self.per_one, self.per_two = table, nodes, per_one, per_two
        self.ones, self.twos = nodes * per_one, nodes * per_two
        self.me, self.row, self.sub = table[0], table[1], table[2]

    def count(self, g):
        return self.table[3 + g]

    def owner(self, h):
        return self.table[3 + self.ones + h]

    def slot(self, h):
        return self.table[3 + self.ones + self.twos + h]

    def ancestor(self, g, a):
        return self.table[3 + self.ones + 2 * self.twos + a * self.ones + g]

    def offset(self, h, t):
        return self.table[3 + (1 + A) * self.ones + (2 + t) * self.twos + h]

    def node(self, k):
        return lax.rem(self.me + k + self.nodes, self.nodes)

    def child(self, node, owner):
        found = jnp.int32(0)
        for c in range(self.per_two):
            found = jnp.where(self.owner(node * self.per_two + c) == owner, c, found)
        return found

    def back(self, block):
        return lax.rem(self.me - block + self.nodes, self.nodes)

    def live(self, g, a):
        return (a < self.count(g)).astype(F32)

    def level_two(self, h):
        h = self.me * self.per_two + h
        parent = self.owner(h) * self.per_one + self.slot(h)
        valid = [(t < 1 + self.count(parent)).astype(F32) for t in range(A)]
        return valid, [self.ancestor(parent, self.offset(h, t)) for t in range(A - 1)]


def fill_rows(out, at, rows, parts):
    for first, part in parts:
        width = part.shape[2]
        for b in range(part.shape[1]):
            out[pl.ds(pl.multiple_of(at + first, rows // 2), part.shape[0]), b * width : (b + 1) * width] = part[:, b, :]


SINGLE, LATE = (1, 3), 2
GROUPS = ((0,), SINGLE, (LATE,))
LONG = 20_000_000_000


def early_kernel(sizes, table, root, own, beside, first, spread, total):
    tree = Tree(table, *sizes)
    per_one, blocks, rows, cols = own.shape
    fill_rows(first, 0, rows, [(0, root)])
    for g in range(per_one):
        for a in range(blocks):
            one = tree.me * per_one + g
            at, valid = tree.ancestor(one, a), tree.live(one, a)
            lanes = slice(g * cols, (g + 1) * cols)
            spread[spot(at * 2 + tree.row, rows), lanes] = own[g, a] * valid
            spread[spot(at * 2 + 1 - tree.row, rows), lanes] = beside[g, a] * valid
    total[...] = mm(first[...], spread[...])


def late_kernel(sizes, table, spread, total, own, across, *refs):
    tree = Tree(table, *sizes)
    shifts = tree.nodes - 1
    far, near = refs[:shifts], refs[shifts : 2 * shifts]
    rest, cov, keep, send, *picks = refs[2 * shifts : 2 * shifts + 4 + tree.nodes]
    wide, tall, part = refs[2 * shifts + 4 + tree.nodes :]
    per_one, blocks, rows, cols = own.shape
    half = rows // 2
    for i in range(shifts):
        fill_rows(rest, i * rows, rows, [(tree.sub * half, far[i]), ((1 - tree.sub) * half, near[i])])
    others = mm(rest[...], spread[...])
    for g in range(per_one):
        lanes = slice(g * cols, (g + 1) * cols)
        tall[g, 0] = total[:, lanes]
        for i in range(shifts):
            tall[g, i + 1] = others[i * rows : (i + 1) * rows, lanes]
    for g in range(per_one):
        one = tree.me * per_one + g
        for a in range(blocks):
            cov[g, a] = tall[g, tree.back(tree.ancestor(one, a))] * (-tree.live(one, a))
    for k in range(tree.nodes):
        target = tree.node(k)
        h = target * tree.per_two + tree.child(target, tree.me)
        for t in range(blocks - 1):
            picks[k][t] = cov[tree.slot(h), tree.offset(h, t)]
    for g in range(per_one):
        one = tree.me * per_one + g
        for a in range(blocks):
            valid = tree.live(one, a)
            wide[a * rows : (a + 1) * rows, spot(tree.sub, cols)] = own[g, a] * valid
            wide[a * rows : (a + 1) * rows, spot(1 - tree.sub, cols)] = across[g, a] * valid
        part[...] = -mm_t(wide[...], cov[g].reshape(blocks * rows, cols))
        keep[g] = part[spot(tree.row, rows), :]
        send[g] = part[spot(1 - tree.row, rows), :]


def diag_one_kernel(sizes, table, diagonal, keep, got, pick, out, *tops):
    tree = Tree(table, *sizes)
    out[...] = diagonal[...] + (keep[...] + got[...])
    for k in range(tree.nodes):
        target = tree.node(k)
        slot = tree.slot(target * tree.per_two + tree.child(target, tree.me))
        if k == LATE:
            tops[k][: A - 1] = pick[...]
            tops[k][A - 1] = out[slot]
        else:
            tops[k][...] = out[slot]


def first_blocks_kernel(sizes, table, panel, later, out):
    soon = panel.shape[0]
    out[:soon] = panel[:, 0]
    out[soon:] = later[:, 0]


def root_two_kernel(sizes, table, first, rest, own, beside, later, across, lower, inner, spread, wide, tall):
    tree = Tree(table, *sizes)
    per_two, blocks, rows, cols = own.shape
    soon = beside.shape[0]
    spread[...] = jnp.zeros_like(spread)
    for h in range(per_two):
        valid, at = tree.level_two(h)
        lanes = slice(h * cols, (h + 1) * cols)
        for t in range(1, blocks):
            spread[spot(at[t - 1] * 2 + tree.row, rows), lanes] = own[h, t] * valid[t]
            spread[spot(at[t - 1] * 2 + 1 - tree.row, rows), lanes] = (beside[h, t] if h < soon else later[h - soon, t]) * valid[t]
    mine = mm(first[...], spread[...])
    others = mm(rest[...], spread[...])
    for h in range(per_two):
        lanes = slice(h * cols, (h + 1) * cols)
        tall[h, 0] = mine[:, lanes]
        for k in range(1, tree.nodes):
            tall[h, k] = others[(k - 1) * rows : k * rows, lanes]
    for h in range(per_two):
        valid, at = tree.level_two(h)
        for t in range(1, blocks):
            lower[h, t - 1] = tall[h, tree.back(at[t - 1])] * valid[t]
            wide[(t - 1) * rows : t * rows, spot(tree.sub, cols)] = own[h, t] * valid[t]
            wide[(t - 1) * rows : t * rows, spot(1 - tree.sub, cols)] = across[h, t] * valid[t]
        inner[h] = mm_t(wide[...], lower[h].reshape((blocks - 1) * rows, cols))


def parent_two_kernel(sizes, shifts, table, own, first_beside, across, corner, lower, inner, diagonal, *refs):
    tree = Tree(table, *sizes)
    row, sub = tree.row, tree.sub
    blocks, rows, cols = own.shape[1:]
    refs = list(refs)
    ins = []
    for k in shifts:
        if k == LATE:
            mine, side = refs[:2]
            del refs[:2]
            ins.append((mine, side, mine.at[A - 1], side.at[A - 1]))
        else:
            ins.append(refs[:4])
            del refs[:4]
    panel, diag, sends, cross, top, first, local, wide, part, more = refs
    low = (blocks - 1) * rows
    for i, k in enumerate(shifts):
        cross_own, cross_side, top_own, top_side = ins[i]
        h = tree.child(tree.me, tree.node(-k))
        valid, _ = tree.level_two(h)
        for t in range(1, blocks):
            span = slice((t - 1) * rows, t * rows)
            cross[span, spot(sub, cols)] = cross_own[t - 1]
            cross[span, spot(1 - sub, cols)] = cross_side[t - 1]
            local[span, :] = own[h, t] * valid[t]
            wide[span, spot(sub, cols)] = own[h, t] * valid[t]
            wide[span, spot(1 - sub, cols)] = across[h, t] * valid[t]
        top[:, spot(sub, cols)] = top_own[...]
        top[:, spot(1 - sub, cols)] = top_side[...]
        first[spot(row, rows), :] = own[h, 0]
        first[spot(1 - row, rows), :] = first_beside[h]
        mine = spot(blocks - 1 + row, rows)
        other = spot(blocks - row, rows)
        wide[mine, spot(sub, cols)] = own[h, 0]
        wide[mine, spot(1 - sub, cols)] = across[h, 0]
        wide[other, spot(sub, cols)] = first_beside[h]
        wide[other, spot(1 - sub, cols)] = corner[h]
        below = mm(cross[...], first[...])
        for t in range(1, blocks):
            span = slice((t - 1) * rows, t * rows)
            part[span, :] = below[span, :] * valid[t]
            panel[i, t] = -(lower[h, t - 1] + part[span, :])
        part[low:, :] = mm_t(cross[...], local[...])
        part[mine, :] += mm(top[...], first[...])
        more[...] = inner[h] + mm_t(wide[...], part[...])
        panel[i, 0] = -part[mine, :]
        sends[i, 0] = part[other, :]
        diag[i] = diagonal[h] + more[spot(row, rows), :]
        sends[i, 1] = more[spot(1 - row, rows), :]


def finish_kernel(sizes, groups, table, *refs):
    tree = Tree(table, *sizes)
    n = len(groups)
    panels, diags, gots = refs[:n], refs[n : 2 * n], refs[2 * n : 3 * n]
    panel_out, diag_out = refs[3 * n :]
    for j, shifts in enumerate(groups):
        for i, k in enumerate(shifts):
            h = tree.child(tree.me, tree.node(-k))
            panel_out[h, 1:] = panels[j][i, 1:]
            panel_out[h, 0] = panels[j][i, 0] - gots[j][i, 0]
            diag_out[h] = diags[j][i] + gots[j][i, 1]


def shift(x, axis, k):
    n = lax.axis_size(axis)
    return lax.ppermute(x, axis, [(i, (i + k) % n) for i in range(n)])


def after(x, *others):
    return lax.optimization_barrier((x,) + others)[0]


def paired_shards(root_inverse, panel_one, diag_one, panel_two, diag_two, ancestors, counts, owners, slots, offsets):
    nodes = lax.axis_size("node")
    me, row, sub = lax.axis_index("node"), lax.axis_index("row"), lax.axis_index("sub")
    per_one, blocks, rows, cols = panel_one.shape
    per_two = panel_two.shape[0]
    sizes = nodes, per_one, per_two
    full = root_inverse.shape[2] * root_inverse.shape[3]
    low = (blocks - 1) * rows
    table = jnp.concatenate(
        [jnp.stack([me, row, sub]).astype(jnp.int32), counts, owners, slots, ancestors.T.reshape(-1), offsets.T.reshape(-1)]
    )
    bind = lambda kernel, *more: functools.partial(kernel, sizes, *more)

    root = root_inverse[0]
    half = lax.dynamic_slice_in_dim(root, sub * (rows // 2), rows // 2, 0)
    far = [shift(half, "node", k) for k in range(1, nodes)]
    beside_one = shift(panel_one, "row", 1)
    soon = per_two // 2
    beside_soon = shift(panel_two[:soon], "row", 1)
    first, spread, total = call(
        bind(early_kernel),
        [array(rows, full), array(full, per_one * cols), array(rows, per_one * cols)],
        table,
        [root, panel_one, beside_one],
    )
    *far, beside_soon, total = lax.optimization_barrier((*far, beside_soon, total))
    near = [shift(x, "sub", 1) for x in far]
    across_one = shift(after(panel_one, total), "sub", 1)
    out = call(
        bind(late_kernel),
        [array((nodes - 1) * rows, full), array(*panel_one.shape), array(per_one, rows, cols), array(per_one, rows, cols)]
        + [array(blocks - 1, rows, cols)] * nodes,
        table,
        [spread, total, panel_one, across_one] + far + near,
        [(blocks * rows, 2 * cols), (per_one, nodes, rows, cols), (2 * rows, cols)],
    )
    rest, cov_panel_one, keep, send = out[:4]
    picks = out[4:]
    got = shift(send, "row", 1)
    beside_later = shift(after(panel_two[soon:], got), "row", 1)
    cross = {k: shift(picks[k], "node", k) for k in SINGLE}
    across_two = shift(after(panel_two, send), "sub", 1)
    out = call(
        bind(diag_one_kernel),
        [array(*diag_one.shape)] + [array(blocks, rows, cols) if k == LATE else array(rows, cols) for k in range(nodes)],
        table,
        [diag_one, keep, got, picks[LATE]],
    )
    cov_diag_one = out[0]
    tops = {k: out[1 + k] if k == 0 else shift(out[1 + k], "node", k) for k in range(nodes)}
    (first_beside,) = call(bind(first_blocks_kernel), [array(per_two, rows, cols)], table, [beside_soon, beside_later])
    corner_two = shift(first_beside, "sub", 1)
    *arrived, panel_early = lax.optimization_barrier((*cross.values(), picks[0], tops[0], panel_two))
    cross_side = [shift(x, "sub", 1) for x in arrived]
    lower, inner = call(
        bind(root_two_kernel),
        [array(per_two, blocks - 1, rows, cols), array(per_two, 2 * rows, cols)],
        table,
        [first, rest, panel_early, beside_soon, beside_later, across_two],
        [(full, per_two * cols), (low, 2 * cols), (per_two, nodes, rows, cols)],
        flops=LONG,
    )
    parent = {0: [arrived[-2], cross_side[-2], arrived[-1], cross_side[-1]]}
    for i, k in enumerate(SINGLE):
        top = after(tops[k], lower)
        parent[k] = [arrived[i], cross_side[i], top, shift(top, "sub", 1)]
    groups = GROUPS
    panels, diags, gots = [], [], []
    for shifts in groups:
        if shifts == (LATE,):
            both = after(tops[LATE], sends)
            parent[LATE] = [both, shift(both, "sub", 1)]
        panel, diag, sends = call(
            bind(parent_two_kernel, shifts),
            [array(len(shifts), blocks, rows, cols), array(len(shifts), rows, cols), array(len(shifts), 2, rows, cols)],
            table,
            [panel_two, first_beside, across_two, corner_two, lower, inner, diag_two]
            + [x for k in shifts for x in parent[k]],
            [
                (low, 2 * cols),
                (rows, 2 * cols),
                (2 * rows, cols),
                (low, cols),
                (low + 2 * rows, 2 * cols),
                (low + 2 * rows, cols),
                (2 * rows, cols),
            ],
        )
        panels.append(panel)
        diags.append(diag)
        gots.append(shift(sends, "row", 1))
    cov_panel_two, cov_diag_two = call(
        bind(finish_kernel, groups),
        [array(*panel_two.shape), array(*diag_two.shape)],
        table,
        panels + diags + gots,
    )
    return (cov_panel_one, cov_diag_one, cov_panel_two, cov_diag_two)


def pick_blocks(gathered, block_ids):
    return gathered[block_ids[:, :, None], :, block_ids[:, None, :]]


def apply_panel(matrix, masked):
    return jnp.einsum(
        "kabic,kbcj->kaij",
        matrix,
        lax.all_gather(masked, "row", axis=2, tiled=True),
        precision=PRECISE,
    )


def diag_update(masked, column, diagonal):
    full_cols = lax.all_gather(masked, "sub", axis=3, tiled=True)
    summed = lax.psum_scatter(
        jnp.einsum("kaij,kail->jkl", full_cols, column, precision=PRECISE),
        "row",
        scatter_dimension=0,
        tiled=True,
    )
    return diagonal - jnp.transpose(summed, (1, 0, 2))


def general_shards(
    root_inverse,
    panel_one,
    diag_one,
    panel_two,
    diag_two,
    ancestors,
    counts,
    owners,
    slots,
    offsets,
):
    nodes = lax.axis_size("node")
    own_index = lax.axis_index("node")
    per_one = panel_one.shape[0]
    per_two = panel_two.shape[0]
    rows_here = panel_one.shape[2]
    width = root_inverse.shape[3]
    positions = jnp.arange(A, dtype=jnp.int32)
    my_ids = lax.dynamic_slice_in_dim(ancestors, own_index * per_one, per_one, 0)
    my_counts = lax.dynamic_slice_in_dim(counts, own_index * per_one, per_one, 0)
    valid_one = (positions[None, :] < my_counts[:, None]).astype(jnp.float32)
    my_owner = lax.dynamic_slice_in_dim(owners, own_index * per_two, per_two, 0)
    my_slot = lax.dynamic_slice_in_dim(slots, own_index * per_two, per_two, 0)
    my_offsets = lax.dynamic_slice_in_dim(offsets, own_index * per_two, per_two, 0)
    my_parent = my_owner * per_one + my_slot
    parent_count = jnp.take(counts, my_parent)
    valid_two = (positions[None, :] < jnp.minimum(A, 1 + parent_count)[:, None]).astype(jnp.float32)
    gathered = lax.all_gather(root_inverse, "node", axis=0, tiled=True)
    block_one = pick_blocks(gathered, my_ids)
    parent_ids = jnp.take_along_axis(jnp.take(ancestors, my_parent, axis=0), my_offsets, axis=1)
    separator = pick_blocks(gathered, parent_ids)
    block_one = block_one * valid_one[:, :, None, None, None]
    masked_one = panel_one * valid_one[:, :, None, None]
    cov_panel_one = -apply_panel(block_one, masked_one)
    cov_diag_one = diag_update(masked_one, cov_panel_one, diag_one)
    full_cross, full_diag = (
        lax.all_gather(cov_panel_one, "sub", axis=3, tiled=True),
        lax.all_gather(cov_diag_one, "sub", axis=2, tiled=True),
    )
    owner_grid = owners.reshape(nodes, per_two)
    child_match = (owner_grid == own_index).astype(jnp.int32)
    has_child = jnp.sum(child_match, axis=1)
    child_pos = jnp.sum(child_match * jnp.arange(per_two, dtype=jnp.int32)[None, :], axis=1)
    child_index = jnp.arange(nodes, dtype=jnp.int32) * per_two + child_pos
    parent_slot = jnp.take(slots, child_index)
    parent_pos = jnp.take(offsets, child_index, axis=0)
    present = has_child.astype(jnp.float32)
    top_send = jnp.take(full_diag, parent_slot, axis=0) * present[:, None, None]
    cross_pick = jnp.take(
        full_cross.reshape(per_one * A, rows_here, width),
        parent_slot[:, None] * A + parent_pos,
        axis=0,
    )
    cross_pick = cross_pick * present[:, None, None, None]
    got_top, got_cross = (
        lax.all_to_all(top_send, "node", split_axis=0, concat_axis=0, tiled=True),
        lax.all_to_all(cross_pick, "node", split_axis=0, concat_axis=0, tiled=True),
    )
    my_cross = jnp.take(got_cross, my_owner, axis=0)
    my_lower = jnp.concatenate([my_cross[:, :, None], separator], axis=2)
    my_top = jnp.take(got_top, my_owner, axis=0)
    empty_blocks = jnp.zeros((per_two, 1, A - 1, rows_here, width), jnp.float32)
    first_row = jnp.concatenate([my_top[:, None, None], empty_blocks], axis=2)
    block_two = jnp.concatenate([first_row, my_lower], axis=1) * valid_two[:, :, None, None, None]
    masked_two = panel_two * valid_two[:, :, None, None]
    lower_part = apply_panel(block_two, masked_two)
    beside = my_lower[:, :, 0]
    further = masked_two[:, 1:]
    upper_part = lax.psum_scatter(
        jnp.einsum("ktci,ktcj->ikj", beside, further, precision=PRECISE),
        "row",
        scatter_dimension=0,
        tiled=True,
    )
    first_block = lower_part[:, 0] + jnp.transpose(upper_part, (1, 0, 2))
    cov_panel_two = -jnp.concatenate([first_block[:, None], lower_part[:, 1:]], axis=1)
    cov_diag_two = diag_update(masked_two, cov_panel_two, diag_two)
    return (cov_panel_one, cov_diag_one, cov_panel_two, cov_diag_two)


def shards(*args):
    sizes = lax.axis_size("node"), lax.axis_size("row"), lax.axis_size("sub")
    root, panel_one, panel_two = args[0], args[1], args[3]
    if sizes == (4, 2, 2) and panel_two.shape[0] == root.shape[2] == panel_one.shape[1] == A and root.shape[0] == 1:
        return paired_shards(*args)
    return general_shards(*args)


def solution(mesh):
    return jax.shard_map(
        shards,
        mesh=mesh,
        in_specs=(
            P(("groups", "node"), "row", None, None),
            P(("groups", "node"), None, "row", "sub"),
            P(("groups", "node"), "row", "sub"),
            P(("groups", "node"), None, "row", "sub"),
            P(("groups", "node"), "row", "sub"),
            P("groups", None),
            P("groups"),
            P("groups"),
            P("groups"),
            P("groups", None),
        ),
        out_specs=(
            P(("groups", "node"), None, "row", "sub"),
            P(("groups", "node"), "row", "sub"),
            P(("groups", "node"), None, "row", "sub"),
            P(("groups", "node"), "row", "sub"),
        ),
        check_vma=False,
    )
```

```python
import functools

import jax
import jax.numpy as jnp
from jax import lax
from jax.experimental import pallas as pl
from jax.experimental.pallas import tpu as pltpu
from jax.sharding import PartitionSpec as P

A = 4


PRECISE = lax.Precision.HIGHEST
THREE_PASS = lax.Precision.HIGH
F32 = jnp.float32
LIMIT = 24 * 1024 * 1024
SMEM = pl.BlockSpec(memory_space=pltpu.SMEM)
VMEM = pl.BlockSpec(memory_space=pltpu.VMEM)


def mm(a, b):
    return jnp.dot(a, b, precision=THREE_PASS, preferred_element_type=F32)


def mm_t(a, b):
    return lax.dot_general(
        a, b, (((0,), (0,)), ((), ())), precision=THREE_PASS, preferred_element_type=F32
    )


def array(*shape):
    return jax.ShapeDtypeStruct(shape, F32)


def call(body, out_shapes, table, operands, scratch=(), flops=0):
    size = sum(4 * o.size for o in operands) + sum(4 * o.size for o in out_shapes)
    return pl.pallas_call(
        body,
        out_shape=tuple(out_shapes),
        in_specs=[SMEM] + [VMEM] * len(operands),
        out_specs=tuple([VMEM] * len(out_shapes)),
        scratch_shapes=[pltpu.VMEM(s, F32) for s in scratch],
        compiler_params=pltpu.CompilerParams(vmem_limit_bytes=LIMIT),
        cost_estimate=pl.CostEstimate(flops=flops, bytes_accessed=0, transcendentals=0),
    )(table, *operands)


def spot(index, size):
    return pl.ds(pl.multiple_of(index * size, size), size)


class Tree:
    def __init__(self, table, nodes, per_one, per_two):
        self.table, self.nodes, self.per_one, self.per_two = table, nodes, per_one, per_two
        self.ones, self.twos = nodes * per_one, nodes * per_two
        self.me, self.row, self.sub = table[0], table[1], table[2]

    def count(self, g):
        return self.table[3 + g]

    def owner(self, h):
        return self.table[3 + self.ones + h]

    def slot(self, h):
        return self.table[3 + self.ones + self.twos + h]

    def ancestor(self, g, a):
        return self.table[3 + self.ones + 2 * self.twos + a * self.ones + g]

    def offset(self, h, t):
        return self.table[3 + (1 + A) * self.ones + (2 + t) * self.twos + h]

    def node(self, k):
        return lax.rem(self.me + k + self.nodes, self.nodes)

    def child(self, node, owner):
        found = jnp.int32(0)
        for c in range(self.per_two):
            found = jnp.where(self.owner(node * self.per_two + c) == owner, c, found)
        return found

    def back(self, block):
        return lax.rem(self.me - block + self.nodes, self.nodes)

    def live(self, g, a):
        return (a < self.count(g)).astype(F32)

    def level_two(self, h):
        h = self.me * self.per_two + h
        parent = self.owner(h) * self.per_one + self.slot(h)
        valid = [(t < 1 + self.count(parent)).astype(F32) for t in range(A)]
        return valid, [self.ancestor(parent, self.offset(h, t)) for t in range(A - 1)]


def fill_rows(out, at, rows, parts):
    for first, part in parts:
        width = part.shape[2]
        for b in range(part.shape[1]):
            out[pl.ds(pl.multiple_of(at + first, rows // 2), part.shape[0]), b * width : (b + 1) * width] = part[:, b, :]


def plain(body, out_shapes, *operands):
    return pl.pallas_call(
        body,
        out_shape=tuple(array(*o.shape) for o in out_shapes),
        in_specs=[VMEM] * len(operands),
        out_specs=tuple([VMEM] * len(out_shapes)),
        compiler_params=pltpu.CompilerParams(vmem_limit_bytes=8 * 1024 * 1024),
    )(*operands)


ORDER = (0, 2, 1, 3)
SPARE = {1: 8, 3: 8}


def early_kernel(sizes, table, root, own, *refs):
    *beside, first, spread, total = refs
    tree = Tree(table, *sizes)
    per_one, blocks, rows, cols = own.shape
    fill_rows(first, 0, rows, [(0, root)])
    for g in range(per_one):
        for a in range(blocks):
            one = tree.me * per_one + g
            at, valid = tree.ancestor(one, a), tree.live(one, a)
            lanes = slice(g * cols, (g + 1) * cols)
            spread[spot(at * 2 + tree.row, rows), lanes] = own[g, a] * valid
            spread[spot(at * 2 + 1 - tree.row, rows), lanes] = beside[g][0, a] * valid
    total[...] = mm(first[...], spread[...])


def level_one_kernel(sizes, table, spread, total, own, across, diagonal, *refs):
    tree = Tree(table, *sizes)
    shifts = tree.nodes - 1
    far, near = refs[:shifts], refs[shifts : 2 * shifts]
    rest, cov, keep, send, *parents = refs[2 * shifts : 2 * shifts + 4 + tree.nodes]
    wide, tall, part = refs[2 * shifts + 4 + tree.nodes :]
    per_one, blocks, rows, cols = own.shape
    half = rows // 2
    for i in range(shifts):
        fill_rows(rest, i * rows, rows, [(tree.sub * half, far[i].at[:half]), ((1 - tree.sub) * half, near[i].at[:half])])
    others = mm(rest[...], spread[...])
    for g in range(per_one):
        lanes = slice(g * cols, (g + 1) * cols)
        tall[g, 0] = total[:, lanes]
        for i in range(shifts):
            tall[g, i + 1] = others[i * rows : (i + 1) * rows, lanes]
    for g in range(per_one):
        one = tree.me * per_one + g
        for a in range(blocks):
            valid = tree.live(one, a)
            cov[g, a] = tall[g, tree.back(tree.ancestor(one, a))] * -valid
            wide[a * rows : (a + 1) * rows, spot(tree.sub, cols)] = own[g, a] * valid
            wide[a * rows : (a + 1) * rows, spot(1 - tree.sub, cols)] = across[g, a] * valid
        part[...] = -mm_t(wide[...], cov[g].reshape(blocks * rows, cols))
        keep[g] = diagonal[g] + part[spot(tree.row, rows), :]
        send[g] = part[spot(1 - tree.row, rows), :]
    for k in range(tree.nodes):
        target = tree.node(k)
        h = target * tree.per_two + tree.child(target, tree.me)
        for t in range(blocks - 1):
            parents[k][t * rows : (t + 1) * rows] = cov[tree.slot(h), tree.offset(h, t)]
        parents[k][(blocks - 1) * rows : blocks * rows] = keep[tree.slot(h)]
        parents[k][blocks * rows : (blocks + 1) * rows] = send[tree.slot(h)]
        if parents[k].shape[0] > (blocks + 1) * rows:
            parents[k][(blocks + 1) * rows :] = jnp.zeros_like(parents[k][(blocks + 1) * rows :])


def add_kernel(keep, got, out):
    out[...] = keep[...] + got[...]


def first_blocks_kernel(panel, out):
    out[...] = panel[:, 0]


def root_two_kernel(sizes, table, first, rest, own, beside, across, lower, inner, spread, wide, tall):
    tree = Tree(table, *sizes)
    per_two, blocks, rows, cols = own.shape
    spread[...] = jnp.zeros_like(spread)
    for h in range(per_two):
        valid, at = tree.level_two(h)
        lanes = slice(h * cols, (h + 1) * cols)
        for t in range(1, blocks):
            spread[spot(at[t - 1] * 2 + tree.row, rows), lanes] = own[h, t] * valid[t]
            spread[spot(at[t - 1] * 2 + 1 - tree.row, rows), lanes] = beside[h, t] * valid[t]
    mine = mm(first[...], spread[...])
    others = mm(rest[...], spread[...])
    for h in range(per_two):
        lanes = slice(h * cols, (h + 1) * cols)
        tall[h, 0] = mine[:, lanes]
        for k in range(1, tree.nodes):
            tall[h, k] = others[(k - 1) * rows : k * rows, lanes]
    for h in range(per_two):
        valid, at = tree.level_two(h)
        for t in range(1, blocks):
            lower[h, t - 1] = tall[h, tree.back(at[t - 1])] * valid[t]
            wide[(t - 1) * rows : t * rows, spot(tree.sub, cols)] = own[h, t] * valid[t]
            wide[(t - 1) * rows : t * rows, spot(1 - tree.sub, cols)] = across[h, t] * valid[t]
        inner[h] = mm_t(wide[...], lower[h].reshape((blocks - 1) * rows, cols))


def parent_two_kernel(sizes, shifts, table, own, beside, across, corner, lower, inner, diagonal, *refs):
    tree = Tree(table, *sizes)
    row, sub = tree.row, tree.sub
    blocks, rows, cols = own.shape[1:]
    n = len(shifts)
    panel, diag, sends, cross, top, first, local, wide, part, more = refs[2 * n :]
    low = (blocks - 1) * rows
    for i, k in enumerate(shifts):
        h = tree.child(tree.me, tree.node(-k))
        valid, _ = tree.level_two(h)
        for got, lanes in (refs[2 * i], spot(sub, cols)), (refs[2 * i + 1], spot(1 - sub, cols)):
            cross[:, lanes] = got[:low]
            top[spot(row, rows), lanes] = got[low : low + rows]
            top[spot(1 - row, rows), lanes] = got[low + rows : low + 2 * rows]
        for t in range(1, blocks):
            span = slice((t - 1) * rows, t * rows)
            local[span, :] = own[h, t] * valid[t]
            wide[span, spot(sub, cols)] = local[span, :]
            wide[span, spot(1 - sub, cols)] = across[h, t] * valid[t]
        first[spot(row, rows), :] = own[h, 0]
        first[spot(1 - row, rows), :] = beside[h]
        mine = spot(blocks - 1 + row, rows)
        other = spot(blocks - row, rows)
        wide[mine, spot(sub, cols)] = own[h, 0]
        wide[mine, spot(1 - sub, cols)] = across[h, 0]
        wide[other, spot(sub, cols)] = beside[h]
        wide[other, spot(1 - sub, cols)] = corner[h]
        below = mm(cross[...], first[...])
        for t in range(1, blocks):
            span = slice((t - 1) * rows, t * rows)
            part[span, :] = below[span, :] * valid[t]
            panel[i, t] = -(lower[h, t - 1] + part[span, :])
        part[low:, :] = mm_t(cross[...], local[...]) + mm(top[...], first[...])
        more[...] = inner[h] + mm_t(wide[...], part[...])
        panel[i, 0] = -part[mine, :]
        sends[i, 0] = part[other, :]
        diag[i] = diagonal[h] + more[spot(row, rows), :]
        sends[i, 1] = more[spot(1 - row, rows), :]


def finish_kernel(sizes, groups, table, *refs):
    tree = Tree(table, *sizes)
    n = len(groups)
    panels, diags, gots = refs[:n], refs[n : 2 * n], refs[2 * n : 3 * n]
    panel_out, diag_out = refs[3 * n :]
    for j, shifts in enumerate(groups):
        for i, k in enumerate(shifts):
            h = tree.child(tree.me, tree.node(-k))
            panel_out[h, 1:] = panels[j][i, 1:]
            panel_out[h, 0] = panels[j][i, 0] - gots[j][i, 0]
            diag_out[h] = diags[j][i] + gots[j][i, 1]


def shift(x, axis, k):
    n = lax.axis_size(axis)
    return lax.ppermute(x, axis, [(i, (i + k) % n) for i in range(n)])


def after(x, *others):
    return lax.optimization_barrier((x,) + others)[0]


def paired_shards(root_inverse, panel_one, diag_one, panel_two, diag_two, ancestors, counts, owners, slots, offsets):
    nodes = lax.axis_size("node")
    me, row, sub = lax.axis_index("node"), lax.axis_index("row"), lax.axis_index("sub")
    per_one, blocks, rows, cols = panel_one.shape
    per_two = panel_two.shape[0]
    sizes = nodes, per_one, per_two
    full = root_inverse.shape[2] * root_inverse.shape[3]
    low = (blocks - 1) * rows
    table = jnp.concatenate(
        [jnp.stack([me, row, sub]).astype(jnp.int32), counts, owners, slots, ancestors.T.reshape(-1), offsets.T.reshape(-1)]
    )
    bind = lambda kernel, *more: functools.partial(kernel, sizes, *more)
    together = lax.optimization_barrier

    half = lax.dynamic_slice_in_dim(root_inverse[0], sub * (rows // 2), rows // 2, 0)
    half = jnp.pad(half, ((0, 2), (0, 0), (0, 0)))
    far = [shift(half, "node", k) for k in range(1, nodes)]
    source = after(panel_one, table)
    beside_one = [shift(source[g : g + 1], "row", 1) for g in range(per_one)]
    first, spread, total = call(
        bind(early_kernel),
        [array(rows, full), array(full, per_one * cols), array(rows, per_one * cols)],
        table,
        [root_inverse[0], panel_one, *beside_one],
    )
    *far, total = together((*far, total))
    near = [shift(x, "sub", 1) for x in far]
    across_one = shift(after(panel_one, far[0]), "sub", 1)
    beside_two = shift(after(panel_two, far[0]), "row", 1)

    rest, cov_panel_one, keep, send, *parents = call(
        bind(level_one_kernel),
        [array((nodes - 1) * rows, full), array(*panel_one.shape), array(per_one, rows, cols), array(per_one, rows, cols)]
        + [array((blocks + 1) * rows + SPARE.get(k, 0), cols) for k in range(nodes)],
        table,
        [spread, total, panel_one, across_one, diag_one] + far + near,
        [(blocks * rows, 2 * cols), (per_one, nodes, rows, cols), (2 * rows, cols)],
    )
    parents = [x if k == 0 else shift(x, "node", k) for k, x in enumerate(parents)]
    across_two = shift(after(panel_two, send), "sub", 1)
    (cov_diag_one,) = plain(add_kernel, [diag_one], keep, shift(send, "row", 1))

    (first_beside,) = plain(first_blocks_kernel, [array(per_two, rows, cols)], beside_two)
    corner_two = shift(first_beside, "sub", 1)
    lower, inner = call(
        bind(root_two_kernel),
        [array(per_two, blocks - 1, rows, cols), array(per_two, 2 * rows, cols)],
        table,
        [first, rest, panel_two, beside_two, across_two],
        [(full, per_two * cols), (low, 2 * cols), (per_two, nodes, rows, cols)],
    )
    panels, diags, gots, waits = [], [], [], []
    for k in ORDER:
        mine = parents[k]
        if k == ORDER[1]:
            mine = after(mine, lower)
        if k in ORDER[2:]:
            mine = after(mine, *waits[:2])
        panel, diag, sends = call(
            bind(parent_two_kernel, (k,)),
            [array(1, blocks, rows, cols), array(1, rows, cols), array(1, 2, rows, cols)],
            table,
            [panel_two, first_beside, across_two, corner_two, lower, inner, diag_two, mine, shift(mine, "sub", 1)],
            [
                (low, 2 * cols),
                (2 * rows, 2 * cols),
                (2 * rows, cols),
                (low, cols),
                (low + 2 * rows, 2 * cols),
                (low + 2 * rows, cols),
                (2 * rows, cols),
            ],
        )
        waits.append(sends)
        panels.append(panel)
        diags.append(diag)
        gots.append(shift(sends, "row", 1))
    cov_panel_two, cov_diag_two = call(
        bind(finish_kernel, tuple((k,) for k in ORDER)),
        [array(*panel_two.shape), array(*diag_two.shape)],
        table,
        panels + diags + gots,
    )
    return (cov_panel_one, cov_diag_one, cov_panel_two, cov_diag_two)


def pick_blocks(gathered, block_ids):
    return gathered[block_ids[:, :, None], :, block_ids[:, None, :]]


def apply_panel(matrix, masked):
    return jnp.einsum(
        "kabic,kbcj->kaij",
        matrix,
        lax.all_gather(masked, "row", axis=2, tiled=True),
        precision=PRECISE,
    )


def diag_update(masked, column, diagonal):
    full_cols = lax.all_gather(masked, "sub", axis=3, tiled=True)
    summed = lax.psum_scatter(
        jnp.einsum("kaij,kail->jkl", full_cols, column, precision=PRECISE),
        "row",
        scatter_dimension=0,
        tiled=True,
    )
    return diagonal - jnp.transpose(summed, (1, 0, 2))


def general_shards(
    root_inverse,
    panel_one,
    diag_one,
    panel_two,
    diag_two,
    ancestors,
    counts,
    owners,
    slots,
    offsets,
):
    nodes = lax.axis_size("node")
    own_index = lax.axis_index("node")
    per_one = panel_one.shape[0]
    per_two = panel_two.shape[0]
    rows_here = panel_one.shape[2]
    width = root_inverse.shape[3]
    positions = jnp.arange(A, dtype=jnp.int32)
    my_ids = lax.dynamic_slice_in_dim(ancestors, own_index * per_one, per_one, 0)
    my_counts = lax.dynamic_slice_in_dim(counts, own_index * per_one, per_one, 0)
    valid_one = (positions[None, :] < my_counts[:, None]).astype(jnp.float32)
    my_owner = lax.dynamic_slice_in_dim(owners, own_index * per_two, per_two, 0)
    my_slot = lax.dynamic_slice_in_dim(slots, own_index * per_two, per_two, 0)
    my_offsets = lax.dynamic_slice_in_dim(offsets, own_index * per_two, per_two, 0)
    my_parent = my_owner * per_one + my_slot
    parent_count = jnp.take(counts, my_parent)
    valid_two = (positions[None, :] < jnp.minimum(A, 1 + parent_count)[:, None]).astype(jnp.float32)
    gathered = lax.all_gather(root_inverse, "node", axis=0, tiled=True)
    block_one = pick_blocks(gathered, my_ids)
    parent_ids = jnp.take_along_axis(jnp.take(ancestors, my_parent, axis=0), my_offsets, axis=1)
    separator = pick_blocks(gathered, parent_ids)
    block_one = block_one * valid_one[:, :, None, None, None]
    masked_one = panel_one * valid_one[:, :, None, None]
    cov_panel_one = -apply_panel(block_one, masked_one)
    cov_diag_one = diag_update(masked_one, cov_panel_one, diag_one)
    full_cross, full_diag = (
        lax.all_gather(cov_panel_one, "sub", axis=3, tiled=True),
        lax.all_gather(cov_diag_one, "sub", axis=2, tiled=True),
    )
    owner_grid = owners.reshape(nodes, per_two)
    child_match = (owner_grid == own_index).astype(jnp.int32)
    has_child = jnp.sum(child_match, axis=1)
    child_pos = jnp.sum(child_match * jnp.arange(per_two, dtype=jnp.int32)[None, :], axis=1)
    child_index = jnp.arange(nodes, dtype=jnp.int32) * per_two + child_pos
    parent_slot = jnp.take(slots, child_index)
    parent_pos = jnp.take(offsets, child_index, axis=0)
    present = has_child.astype(jnp.float32)
    top_send = jnp.take(full_diag, parent_slot, axis=0) * present[:, None, None]
    cross_pick = jnp.take(
        full_cross.reshape(per_one * A, rows_here, width),
        parent_slot[:, None] * A + parent_pos,
        axis=0,
    )
    cross_pick = cross_pick * present[:, None, None, None]
    got_top, got_cross = (
        lax.all_to_all(top_send, "node", split_axis=0, concat_axis=0, tiled=True),
        lax.all_to_all(cross_pick, "node", split_axis=0, concat_axis=0, tiled=True),
    )
    my_cross = jnp.take(got_cross, my_owner, axis=0)
    my_lower = jnp.concatenate([my_cross[:, :, None], separator], axis=2)
    my_top = jnp.take(got_top, my_owner, axis=0)
    empty_blocks = jnp.zeros((per_two, 1, A - 1, rows_here, width), jnp.float32)
    first_row = jnp.concatenate([my_top[:, None, None], empty_blocks], axis=2)
    block_two = jnp.concatenate([first_row, my_lower], axis=1) * valid_two[:, :, None, None, None]
    masked_two = panel_two * valid_two[:, :, None, None]
    lower_part = apply_panel(block_two, masked_two)
    beside = my_lower[:, :, 0]
    further = masked_two[:, 1:]
    upper_part = lax.psum_scatter(
        jnp.einsum("ktci,ktcj->ikj", beside, further, precision=PRECISE),
        "row",
        scatter_dimension=0,
        tiled=True,
    )
    first_block = lower_part[:, 0] + jnp.transpose(upper_part, (1, 0, 2))
    cov_panel_two = -jnp.concatenate([first_block[:, None], lower_part[:, 1:]], axis=1)
    cov_diag_two = diag_update(masked_two, cov_panel_two, diag_two)
    return (cov_panel_one, cov_diag_one, cov_panel_two, cov_diag_two)


def shards(*args):
    sizes = lax.axis_size("node"), lax.axis_size("row"), lax.axis_size("sub")
    root, panel_one, panel_two = args[0], args[1], args[3]
    if sizes == (4, 2, 2) and panel_two.shape[0] == root.shape[2] == panel_one.shape[1] == A and root.shape[0] == 1:
        return paired_shards(*args)
    return general_shards(*args)


def solution(mesh):
    return jax.shard_map(
        shards,
        mesh=mesh,
        in_specs=(
            P(("groups", "node"), "row", None, None),
            P(("groups", "node"), None, "row", "sub"),
            P(("groups", "node"), "row", "sub"),
            P(("groups", "node"), None, "row", "sub"),
            P(("groups", "node"), "row", "sub"),
            P("groups", None),
            P("groups"),
            P("groups"),
            P("groups"),
            P("groups", None),
        ),
        out_specs=(
            P(("groups", "node"), None, "row", "sub"),
            P(("groups", "node"), "row", "sub"),
            P(("groups", "node"), None, "row", "sub"),
            P(("groups", "node"), "row", "sub"),
        ),
        check_vma=False,
    )
```

```python
import functools

import jax
import jax.numpy as jnp
from jax import lax
from jax.experimental import pallas as pl
from jax.experimental.pallas import tpu as pltpu
from jax.sharding import PartitionSpec as P

A = 4


PRECISE = lax.Precision.HIGHEST
THREE_PASS = lax.Precision.HIGH
F32 = jnp.float32
LIMIT = 24 * 1024 * 1024
SMEM = pl.BlockSpec(memory_space=pltpu.SMEM)
VMEM = pl.BlockSpec(memory_space=pltpu.VMEM)


def mm(a, b):
    return jnp.dot(a, b, precision=THREE_PASS, preferred_element_type=F32)


def mm_t(a, b):
    return lax.dot_general(
        a, b, (((0,), (0,)), ((), ())), precision=THREE_PASS, preferred_element_type=F32
    )


def array(*shape):
    return jax.ShapeDtypeStruct(shape, F32)


def call(body, out_shapes, table, operands, scratch=(), flops=0):
    size = sum(4 * o.size for o in operands) + sum(4 * o.size for o in out_shapes)
    return pl.pallas_call(
        body,
        out_shape=tuple(out_shapes),
        in_specs=[SMEM] + [VMEM] * len(operands),
        out_specs=tuple([VMEM] * len(out_shapes)),
        scratch_shapes=[pltpu.VMEM(s, F32) for s in scratch],
        compiler_params=pltpu.CompilerParams(vmem_limit_bytes=LIMIT),
        cost_estimate=pl.CostEstimate(flops=flops, bytes_accessed=0, transcendentals=0),
    )(table, *operands)


def spot(index, size):
    return pl.ds(pl.multiple_of(index * size, size), size)


class Tree:
    def __init__(self, table, nodes, per_one, per_two):
        self.table, self.nodes, self.per_one, self.per_two = table, nodes, per_one, per_two
        self.ones, self.twos = nodes * per_one, nodes * per_two
        self.me, self.row, self.sub = table[0], table[1], table[2]

    def count(self, g):
        return self.table[3 + g]

    def owner(self, h):
        return self.table[3 + self.ones + h]

    def slot(self, h):
        return self.table[3 + self.ones + self.twos + h]

    def ancestor(self, g, a):
        return self.table[3 + self.ones + 2 * self.twos + a * self.ones + g]

    def offset(self, h, t):
        return self.table[3 + (1 + A) * self.ones + (2 + t) * self.twos + h]

    def node(self, k):
        return lax.rem(self.me + k + self.nodes, self.nodes)

    def child(self, node, owner):
        found = jnp.int32(0)
        for c in range(self.per_two):
            found = jnp.where(self.owner(node * self.per_two + c) == owner, c, found)
        return found

    def back(self, block):
        return lax.rem(self.me - block + self.nodes, self.nodes)

    def live(self, g, a):
        return (a < self.count(g)).astype(F32)

    def level_two(self, h):
        h = self.me * self.per_two + h
        parent = self.owner(h) * self.per_one + self.slot(h)
        valid = [(t < 1 + self.count(parent)).astype(F32) for t in range(A)]
        return valid, [self.ancestor(parent, self.offset(h, t)) for t in range(A - 1)]


def fill_rows(out, at, rows, parts):
    for first, part in parts:
        width = part.shape[2]
        for b in range(part.shape[1]):
            out[pl.ds(pl.multiple_of(at + first, rows // 2), part.shape[0]), b * width : (b + 1) * width] = part[:, b, :]


def plain(body, out_shapes, *operands):
    return pl.pallas_call(
        body,
        out_shape=tuple(array(*o.shape) for o in out_shapes),
        in_specs=[VMEM] * len(operands),
        out_specs=tuple([VMEM] * len(out_shapes)),
        compiler_params=pltpu.CompilerParams(vmem_limit_bytes=8 * 1024 * 1024),
    )(*operands)


ORDER = (0, 2, 1, 3)
SPARE = {1: 8, 3: 8}


def early_kernel(sizes, table, root, own, *refs):
    *beside, first, spread, total = refs
    tree = Tree(table, *sizes)
    per_one, blocks, rows, cols = own.shape
    fill_rows(first, 0, rows, [(0, root)])
    for g in range(per_one):
        for a in range(blocks):
            one = tree.me * per_one + g
            at, valid = tree.ancestor(one, a), tree.live(one, a)
            lanes = slice(g * cols, (g + 1) * cols)
            spread[spot(at * 2 + tree.row, rows), lanes] = own[g, a] * valid
            spread[spot(at * 2 + 1 - tree.row, rows), lanes] = beside[g][0, a] * valid
    total[...] = mm(first[...], spread[...])


def level_one_kernel(sizes, table, spread, total, own, across, diagonal, *refs):
    tree = Tree(table, *sizes)
    shifts = tree.nodes - 1
    far, near = refs[:shifts], refs[shifts : 2 * shifts]
    rest, cov, keep, send, *parents = refs[2 * shifts : 2 * shifts + 4 + tree.nodes]
    wide, tall, part = refs[2 * shifts + 4 + tree.nodes :]
    per_one, blocks, rows, cols = own.shape
    half = rows // 2
    for i in range(shifts):
        fill_rows(rest, i * rows, rows, [(tree.sub * half, far[i].at[:half]), ((1 - tree.sub) * half, near[i].at[:half])])
    others = mm(rest[...], spread[...])
    for g in range(per_one):
        lanes = slice(g * cols, (g + 1) * cols)
        tall[g, 0] = total[:, lanes]
        for i in range(shifts):
            tall[g, i + 1] = others[i * rows : (i + 1) * rows, lanes]
    for g in range(per_one):
        one = tree.me * per_one + g
        for a in range(blocks):
            valid = tree.live(one, a)
            cov[g, a] = tall[g, tree.back(tree.ancestor(one, a))] * -valid
            wide[a * rows : (a + 1) * rows, spot(tree.sub, cols)] = own[g, a] * valid
            wide[a * rows : (a + 1) * rows, spot(1 - tree.sub, cols)] = across[g, a] * valid
        part[...] = -mm_t(wide[...], cov[g].reshape(blocks * rows, cols))
        keep[g] = diagonal[g] + part[spot(tree.row, rows), :]
        send[g] = part[spot(1 - tree.row, rows), :]
    for k in range(tree.nodes):
        target = tree.node(k)
        h = target * tree.per_two + tree.child(target, tree.me)
        for t in range(blocks - 1):
            parents[k][t * rows : (t + 1) * rows] = cov[tree.slot(h), tree.offset(h, t)]
        parents[k][(blocks - 1) * rows : blocks * rows] = keep[tree.slot(h)]
        parents[k][blocks * rows : (blocks + 1) * rows] = send[tree.slot(h)]
        if parents[k].shape[0] > (blocks + 1) * rows:
            parents[k][(blocks + 1) * rows :] = jnp.zeros_like(parents[k][(blocks + 1) * rows :])


def first_blocks_kernel(panel, out):
    for h in range(out.shape[0]):
        start = A * h * out.shape[1]
        out[h] = panel[start : start + out.shape[1]]


def prepare_two_kernel(sizes, table, first, rest, own, across, mine, others, turned, near_rows, spread, wide):
    tree = Tree(table, *sizes)
    row, sub = tree.row, tree.sub
    per_two, blocks, rows, cols = own.shape
    for b in range(first.shape[1] // (2 * rows)):
        lanes = slice(b * rows, (b + 1) * rows)
        for out, half in (near_rows, row), (others, 1 - row):
            out[:rows, lanes] = first[:, spot(2 * b + half, rows)]
            out[rows:, lanes] = rest[:, spot(2 * b + half, rows)]
    spread[...] = jnp.zeros_like(spread)
    for h in range(per_two):
        valid, at = tree.level_two(h)
        for t in range(1, blocks):
            span = slice((t - 1) * rows, t * rows)
            spread[spot(at[t - 1], rows), h * cols : (h + 1) * cols] = own[h, t] * valid[t]
            wide[span, spot(sub, cols)] = own[h, t] * valid[t]
            wide[span, spot(1 - sub, cols)] = across[h, t] * valid[t]
        wide[(blocks - 1) * rows :, spot(sub, cols)] = own[h, 0]
        wide[(blocks - 1) * rows :, spot(1 - sub, cols)] = across[h, 0]
        turned[h] = wide[...].T
    mine[...] = mm(near_rows[...], spread[...])


def root_two_kernel(sizes, table, mine, others, turned, beside, lower, inner, spread, tall):
    tree = Tree(table, *sizes)
    per_two, rows, cols = lower.shape[0], lower.shape[2], lower.shape[3]
    blocks = lower.shape[1] + 1
    spread[...] = jnp.zeros_like(spread)
    for h in range(per_two):
        valid, at = tree.level_two(h)
        for t in range(1, blocks):
            spread[spot(at[t - 1], rows), h * cols : (h + 1) * cols] = beside[(blocks * h + t) * rows : (blocks * h + t + 1) * rows] * valid[t]
    total = mine[...] + mm(others[...], spread[...])
    for h in range(per_two):
        for k in range(tree.nodes):
            tall[h, k] = total[k * rows : (k + 1) * rows, h * cols : (h + 1) * cols]
    for h in range(per_two):
        valid, at = tree.level_two(h)
        for t in range(1, blocks):
            lower[h, t - 1] = tall[h, tree.back(at[t - 1])] * valid[t]
        inner[h] = mm(turned[h, :, : (blocks - 1) * rows], lower[h].reshape((blocks - 1) * rows, cols))


def parent_two_kernel(sizes, shifts, table, own, beside, corner, turned, lower, inner, diagonal, *refs):
    tree = Tree(table, *sizes)
    row, sub = tree.row, tree.sub
    blocks, rows, cols = own.shape[1:]
    n = len(shifts)
    panel, diag, sends, cross, top, first, far, part, lead, more = refs[2 * n :]
    low = (blocks - 1) * rows
    for i, k in enumerate(shifts):
        h = tree.child(tree.me, tree.node(-k))
        valid, _ = tree.level_two(h)
        for got, lanes in (refs[2 * i], spot(sub, cols)), (refs[2 * i + 1], spot(1 - sub, cols)):
            cross[:, lanes] = got[:low]
            top[spot(row, rows), lanes] = got[low : low + rows]
            top[spot(1 - row, rows), lanes] = got[low + rows : low + 2 * rows]
        first[spot(row, rows), :] = own[h, 0]
        first[spot(1 - row, rows), :] = beside[h]
        far[:, spot(sub, cols)] = beside[h]
        far[:, spot(1 - sub, cols)] = corner[h]
        below = mm(cross[...], first[...])
        for t in range(1, blocks):
            span = slice((t - 1) * rows, t * rows)
            part[span, :] = below[span, :] * valid[t]
            panel[i, t] = -(lower[h, t - 1] + part[span, :])
        lead[...] = mm(turned[h, spot(sub, cols), :low], cross[...]).T + mm(top[...], first[...])
        mine, other = lead[spot(row, rows), :], lead[spot(1 - row, rows), :]
        part[low:, :] = mine
        more[...] = inner[h] + mm(turned[h], part[...]) + mm_t(far[...], other)
        panel[i, 0] = -mine
        sends[i, 0] = other
        diag[i] = diagonal[h] + more[spot(row, rows), :]
        sends[i, 1] = more[spot(1 - row, rows), :]


def finish_kernel(sizes, groups, table, *refs):
    tree = Tree(table, *sizes)
    n = len(groups)
    panels, diags, gots = refs[:n], refs[n : 2 * n], refs[2 * n : 3 * n]
    keep, got_one, panel_out, diag_out, one_out = refs[3 * n :]
    one_out[...] = keep[...] + got_one[...]
    for j, shifts in enumerate(groups):
        for i, k in enumerate(shifts):
            h = tree.child(tree.me, tree.node(-k))
            panel_out[h, 1:] = panels[j][i, 1:]
            panel_out[h, 0] = panels[j][i, 0] - gots[j][i, 0]
            diag_out[h] = diags[j][i] + gots[j][i, 1]


def shift(x, axis, k):
    n = lax.axis_size(axis)
    return lax.ppermute(x, axis, [(i, (i + k) % n) for i in range(n)])


def after(x, *others):
    return lax.optimization_barrier((x,) + others)[0]


def paired_shards(root_inverse, panel_one, diag_one, panel_two, diag_two, ancestors, counts, owners, slots, offsets):
    nodes = lax.axis_size("node")
    me, row, sub = lax.axis_index("node"), lax.axis_index("row"), lax.axis_index("sub")
    per_one, blocks, rows, cols = panel_one.shape
    per_two = panel_two.shape[0]
    sizes = nodes, per_one, per_two
    full = root_inverse.shape[2] * root_inverse.shape[3]
    low = (blocks - 1) * rows
    table = jnp.concatenate(
        [jnp.stack([me, row, sub]).astype(jnp.int32), counts, owners, slots, ancestors.T.reshape(-1), offsets.T.reshape(-1)]
    )
    bind = lambda kernel, *more: functools.partial(kernel, sizes, *more)
    together = lax.optimization_barrier

    half = lax.dynamic_slice_in_dim(root_inverse[0], sub * (rows // 2), rows // 2, 0)
    half = jnp.pad(half, ((0, 2), (0, 0), (0, 0)))
    far = [shift(half, "node", k) for k in range(1, nodes)]
    source = after(panel_one, table)
    beside_one = [shift(source[g : g + 1], "row", 1) for g in range(per_one)]
    first, spread, total = call(
        bind(early_kernel),
        [array(rows, full), array(full, per_one * cols), array(rows, per_one * cols)],
        table,
        [root_inverse[0], panel_one, *beside_one],
    )
    *far, total = together((*far, total))
    near = [shift(x, "sub", 1) for x in far]
    across_one = shift(after(panel_one, far[0]), "sub", 1)
    flat = jnp.pad(panel_two.reshape(per_two * blocks * rows, cols), ((0, 16), (0, 0)))
    beside_two = shift(after(flat, far[0]), "row", 1)

    rest, cov_panel_one, keep, send, *parents = call(
        bind(level_one_kernel),
        [array((nodes - 1) * rows, full), array(*panel_one.shape), array(per_one, rows, cols), array(per_one, rows, cols)]
        + [array((blocks + 1) * rows + SPARE.get(k, 0), cols) for k in range(nodes)],
        table,
        [spread, total, panel_one, across_one, diag_one] + far + near,
        [(blocks * rows, 2 * cols), (per_one, nodes, rows, cols), (2 * rows, cols)],
    )
    parents = [x if k == 0 else shift(x, "node", k) for k, x in enumerate(parents)]
    got_one = shift(send, "row", 1)
    across_two = shift(after(panel_two, send), "sub", 1)

    own_part, others, turned = call(
        bind(prepare_two_kernel),
        [array(nodes * rows, per_two * cols), array(nodes * rows, full // 2), array(per_two, 2 * rows, low + rows)],
        table,
        [first, rest, panel_two, across_two],
        [(nodes * rows, full // 2), (full // 2, per_two * cols), (low + rows, 2 * cols)],
    )
    beside_two, own_part = together((beside_two, own_part))
    (first_beside,) = plain(first_blocks_kernel, [array(per_two, rows, cols)], beside_two)
    corner_two = shift(first_beside, "sub", 1)
    lower, inner = call(
        bind(root_two_kernel),
        [array(per_two, blocks - 1, rows, cols), array(per_two, 2 * rows, cols)],
        table,
        [own_part, others, turned, beside_two],
        [(full // 2, per_two * cols), (per_two, nodes, rows, cols)],
    )
    panels, diags, gots, sent = [], [], [], []
    for k in ORDER:
        mine = parents[k]
        if k == ORDER[1]:
            mine = after(mine, lower)
        if k in ORDER[2:]:
            mine = after(mine, *sent[:2])
        side = shift(mine, "sub", 1)
        if k == ORDER[1]:
            mine = after(mine, got_one)
        panel, diag, sends = call(
            bind(parent_two_kernel, (k,)),
            [array(1, blocks, rows, cols), array(1, rows, cols), array(1, 2, rows, cols)],
            table,
            [panel_two, first_beside, corner_two, turned, lower, inner, diag_two, mine, side],
            [
                (low, 2 * cols),
                (2 * rows, 2 * cols),
                (2 * rows, cols),
                (rows, 2 * cols),
                (low + rows, cols),
                (2 * rows, cols),
                (2 * rows, cols),
            ],
        )
        sent.append(sends)
        panels.append(panel)
        diags.append(diag)
        gots.append(shift(sends, "row", 1))
    cov_panel_two, cov_diag_two, cov_diag_one = call(
        bind(finish_kernel, tuple((k,) for k in ORDER)),
        [array(*panel_two.shape), array(*diag_two.shape), array(*diag_one.shape)],
        table,
        panels + diags + gots + [keep, got_one],
    )
    return (cov_panel_one, cov_diag_one, cov_panel_two, cov_diag_two)


def pick_blocks(gathered, block_ids):
    return gathered[block_ids[:, :, None], :, block_ids[:, None, :]]


def apply_panel(matrix, masked):
    return jnp.einsum(
        "kabic,kbcj->kaij",
        matrix,
        lax.all_gather(masked, "row", axis=2, tiled=True),
        precision=PRECISE,
    )


def diag_update(masked, column, diagonal):
    full_cols = lax.all_gather(masked, "sub", axis=3, tiled=True)
    summed = lax.psum_scatter(
        jnp.einsum("kaij,kail->jkl", full_cols, column, precision=PRECISE),
        "row",
        scatter_dimension=0,
        tiled=True,
    )
    return diagonal - jnp.transpose(summed, (1, 0, 2))


def general_shards(
    root_inverse,
    panel_one,
    diag_one,
    panel_two,
    diag_two,
    ancestors,
    counts,
    owners,
    slots,
    offsets,
):
    nodes = lax.axis_size("node")
    own_index = lax.axis_index("node")
    per_one = panel_one.shape[0]
    per_two = panel_two.shape[0]
    rows_here = panel_one.shape[2]
    width = root_inverse.shape[3]
    positions = jnp.arange(A, dtype=jnp.int32)
    my_ids = lax.dynamic_slice_in_dim(ancestors, own_index * per_one, per_one, 0)
    my_counts = lax.dynamic_slice_in_dim(counts, own_index * per_one, per_one, 0)
    valid_one = (positions[None, :] < my_counts[:, None]).astype(jnp.float32)
    my_owner = lax.dynamic_slice_in_dim(owners, own_index * per_two, per_two, 0)
    my_slot = lax.dynamic_slice_in_dim(slots, own_index * per_two, per_two, 0)
    my_offsets = lax.dynamic_slice_in_dim(offsets, own_index * per_two, per_two, 0)
    my_parent = my_owner * per_one + my_slot
    parent_count = jnp.take(counts, my_parent)
    valid_two = (positions[None, :] < jnp.minimum(A, 1 + parent_count)[:, None]).astype(jnp.float32)
    gathered = lax.all_gather(root_inverse, "node", axis=0, tiled=True)
    block_one = pick_blocks(gathered, my_ids)
    parent_ids = jnp.take_along_axis(jnp.take(ancestors, my_parent, axis=0), my_offsets, axis=1)
    separator = pick_blocks(gathered, parent_ids)
    block_one = block_one * valid_one[:, :, None, None, None]
    masked_one = panel_one * valid_one[:, :, None, None]
    cov_panel_one = -apply_panel(block_one, masked_one)
    cov_diag_one = diag_update(masked_one, cov_panel_one, diag_one)
    full_cross, full_diag = (
        lax.all_gather(cov_panel_one, "sub", axis=3, tiled=True),
        lax.all_gather(cov_diag_one, "sub", axis=2, tiled=True),
    )
    owner_grid = owners.reshape(nodes, per_two)
    child_match = (owner_grid == own_index).astype(jnp.int32)
    has_child = jnp.sum(child_match, axis=1)
    child_pos = jnp.sum(child_match * jnp.arange(per_two, dtype=jnp.int32)[None, :], axis=1)
    child_index = jnp.arange(nodes, dtype=jnp.int32) * per_two + child_pos
    parent_slot = jnp.take(slots, child_index)
    parent_pos = jnp.take(offsets, child_index, axis=0)
    present = has_child.astype(jnp.float32)
    top_send = jnp.take(full_diag, parent_slot, axis=0) * present[:, None, None]
    cross_pick = jnp.take(
        full_cross.reshape(per_one * A, rows_here, width),
        parent_slot[:, None] * A + parent_pos,
        axis=0,
    )
    cross_pick = cross_pick * present[:, None, None, None]
    got_top, got_cross = (
        lax.all_to_all(top_send, "node", split_axis=0, concat_axis=0, tiled=True),
        lax.all_to_all(cross_pick, "node", split_axis=0, concat_axis=0, tiled=True),
    )
    my_cross = jnp.take(got_cross, my_owner, axis=0)
    my_lower = jnp.concatenate([my_cross[:, :, None], separator], axis=2)
    my_top = jnp.take(got_top, my_owner, axis=0)
    empty_blocks = jnp.zeros((per_two, 1, A - 1, rows_here, width), jnp.float32)
    first_row = jnp.concatenate([my_top[:, None, None], empty_blocks], axis=2)
    block_two = jnp.concatenate([first_row, my_lower], axis=1) * valid_two[:, :, None, None, None]
    masked_two = panel_two * valid_two[:, :, None, None]
    lower_part = apply_panel(block_two, masked_two)
    beside = my_lower[:, :, 0]
    further = masked_two[:, 1:]
    upper_part = lax.psum_scatter(
        jnp.einsum("ktci,ktcj->ikj", beside, further, precision=PRECISE),
        "row",
        scatter_dimension=0,
        tiled=True,
    )
    first_block = lower_part[:, 0] + jnp.transpose(upper_part, (1, 0, 2))
    cov_panel_two = -jnp.concatenate([first_block[:, None], lower_part[:, 1:]], axis=1)
    cov_diag_two = diag_update(masked_two, cov_panel_two, diag_two)
    return (cov_panel_one, cov_diag_one, cov_panel_two, cov_diag_two)


def shards(*args):
    sizes = lax.axis_size("node"), lax.axis_size("row"), lax.axis_size("sub")
    root, panel_one, panel_two = args[0], args[1], args[3]
    if sizes == (4, 2, 2) and panel_two.shape[0] == root.shape[2] == panel_one.shape[1] == A and root.shape[0] == 1:
        return paired_shards(*args)
    return general_shards(*args)


def solution(mesh):
    return jax.shard_map(
        shards,
        mesh=mesh,
        in_specs=(
            P(("groups", "node"), "row", None, None),
            P(("groups", "node"), None, "row", "sub"),
            P(("groups", "node"), "row", "sub"),
            P(("groups", "node"), None, "row", "sub"),
            P(("groups", "node"), "row", "sub"),
            P("groups", None),
            P("groups"),
            P("groups"),
            P("groups"),
            P("groups", None),
        ),
        out_specs=(
            P(("groups", "node"), None, "row", "sub"),
            P(("groups", "node"), "row", "sub"),
            P(("groups", "node"), None, "row", "sub"),
            P(("groups", "node"), "row", "sub"),
        ),
        check_vma=False,
    )
```

```python
import functools

import jax
import jax.numpy as jnp
from jax import lax
from jax.experimental import pallas as pl
from jax.experimental.pallas import tpu as pltpu
from jax.sharding import PartitionSpec as P

A = 4


PRECISE = lax.Precision.HIGHEST
THREE_PASS = lax.Precision.HIGH
F32 = jnp.float32
LIMIT = 24 * 1024 * 1024
SMEM = pl.BlockSpec(memory_space=pltpu.SMEM)
VMEM = pl.BlockSpec(memory_space=pltpu.VMEM)


def mm(a, b):
    return jnp.dot(a, b, precision=THREE_PASS, preferred_element_type=F32)


def mm_t(a, b):
    return lax.dot_general(
        a, b, (((0,), (0,)), ((), ())), precision=THREE_PASS, preferred_element_type=F32
    )


def array(*shape):
    return jax.ShapeDtypeStruct(shape, F32)


def call(body, out_shapes, table, operands, scratch=(), flops=0):
    size = sum(4 * o.size for o in operands) + sum(4 * o.size for o in out_shapes)
    return pl.pallas_call(
        body,
        out_shape=tuple(out_shapes),
        in_specs=[SMEM] + [VMEM] * len(operands),
        out_specs=tuple([VMEM] * len(out_shapes)),
        scratch_shapes=[pltpu.VMEM(s, F32) for s in scratch],
        compiler_params=pltpu.CompilerParams(vmem_limit_bytes=LIMIT),
        cost_estimate=pl.CostEstimate(flops=flops, bytes_accessed=0, transcendentals=0),
    )(table, *operands)


def spot(index, size):
    return pl.ds(pl.multiple_of(index * size, size), size)


class Tree:
    def __init__(self, table, nodes, per_one, per_two):
        self.table, self.nodes, self.per_one, self.per_two = table, nodes, per_one, per_two
        self.ones, self.twos = nodes * per_one, nodes * per_two
        self.me, self.row, self.sub = table[0], table[1], table[2]

    def count(self, g):
        return self.table[3 + g]

    def owner(self, h):
        return self.table[3 + self.ones + h]

    def slot(self, h):
        return self.table[3 + self.ones + self.twos + h]

    def ancestor(self, g, a):
        return self.table[3 + self.ones + 2 * self.twos + a * self.ones + g]

    def offset(self, h, t):
        return self.table[3 + (1 + A) * self.ones + (2 + t) * self.twos + h]

    def node(self, k):
        return lax.rem(self.me + k + self.nodes, self.nodes)

    def child(self, node, owner):
        found = jnp.int32(0)
        for c in range(self.per_two):
            found = jnp.where(self.owner(node * self.per_two + c) == owner, c, found)
        return found

    def back(self, block):
        return lax.rem(self.me - block + self.nodes, self.nodes)

    def live(self, g, a):
        return (a < self.count(g)).astype(F32)

    def level_two(self, h):
        h = self.me * self.per_two + h
        parent = self.owner(h) * self.per_one + self.slot(h)
        valid = [(t < 1 + self.count(parent)).astype(F32) for t in range(A)]
        return valid, [self.ancestor(parent, self.offset(h, t)) for t in range(A - 1)]


def fill_rows(out, at, rows, parts):
    for first, part in parts:
        if len(part.shape) == 2:
            high, wide = rows // 2, part.shape[1]
            for c in range(out.shape[1] // wide):
                out[pl.ds(pl.multiple_of(at + first, high), high), c * wide : (c + 1) * wide] = part[c * high : (c + 1) * high]
            continue
        width = part.shape[2]
        for b in range(part.shape[1]):
            out[pl.ds(pl.multiple_of(at + first, rows // 2), part.shape[0]), b * width : (b + 1) * width] = part[:, b, :]


def plain(body, out_shapes, *operands):
    return pl.pallas_call(
        body,
        out_shape=tuple(array(*o.shape) for o in out_shapes),
        in_specs=[VMEM] * len(operands),
        out_specs=tuple([VMEM] * len(out_shapes)),
        compiler_params=pltpu.CompilerParams(vmem_limit_bytes=8 * 1024 * 1024),
    )(*operands)


ORDER = (0, 2, 1, 3)
SPARE = {1: 8, 3: 8}


def early_kernel(sizes, table, root, own, *refs):
    *beside, first, spread, total = refs
    tree = Tree(table, *sizes)
    per_one, blocks, rows, cols = own.shape
    fill_rows(first, 0, rows, [(0, root)])
    for g in range(per_one):
        for a in range(blocks):
            one = tree.me * per_one + g
            at, valid = tree.ancestor(one, a), tree.live(one, a)
            lanes = slice(g * cols, (g + 1) * cols)
            spread[spot(at * 2 + tree.row, rows), lanes] = own[g, a] * valid
            spread[spot(at * 2 + 1 - tree.row, rows), lanes] = beside[g][0, a] * valid
    total[...] = mm(first[...], spread[...])


def level_one_kernel(sizes, table, spread, total, own, across, diagonal, *refs):
    tree = Tree(table, *sizes)
    shifts = tree.nodes - 1
    far, near = refs[:shifts], refs[shifts : 2 * shifts]
    rest, cov, keep, send, *parents = refs[2 * shifts : 2 * shifts + 4 + tree.nodes]
    wide, tall, part = refs[2 * shifts + 4 + tree.nodes :]
    per_one, blocks, rows, cols = own.shape
    half = rows // 2
    for i in range(shifts):
        fill_rows(rest, i * rows, rows, [(tree.sub * half, far[i]), ((1 - tree.sub) * half, near[i])])
    others = mm(rest[...], spread[...])
    for g in range(per_one):
        lanes = slice(g * cols, (g + 1) * cols)
        tall[g, 0] = total[:, lanes]
        for i in range(shifts):
            tall[g, i + 1] = others[i * rows : (i + 1) * rows, lanes]
    for g in range(per_one):
        one = tree.me * per_one + g
        for a in range(blocks):
            valid = tree.live(one, a)
            cov[g, a] = tall[g, tree.back(tree.ancestor(one, a))] * -valid
            wide[a * rows : (a + 1) * rows, spot(tree.sub, cols)] = own[g, a] * valid
            wide[a * rows : (a + 1) * rows, spot(1 - tree.sub, cols)] = across[g, a] * valid
        part[...] = -mm_t(wide[...], cov[g].reshape(blocks * rows, cols))
        keep[g] = diagonal[g] + part[spot(tree.row, rows), :]
        send[g] = part[spot(1 - tree.row, rows), :]
    for k in range(tree.nodes):
        target = tree.node(k)
        h = target * tree.per_two + tree.child(target, tree.me)
        for t in range(blocks - 1):
            parents[k][t * rows : (t + 1) * rows] = cov[tree.slot(h), tree.offset(h, t)]
        parents[k][(blocks - 1) * rows : blocks * rows] = keep[tree.slot(h)]
        parents[k][blocks * rows : (blocks + 1) * rows] = send[tree.slot(h)]
        if parents[k].shape[0] > (blocks + 1) * rows:
            parents[k][(blocks + 1) * rows :] = jnp.zeros_like(parents[k][(blocks + 1) * rows :])


def first_blocks_kernel(panel, out):
    for h in range(out.shape[0]):
        start = A * h * out.shape[1]
        out[h] = panel[start : start + out.shape[1]]


def prepare_two_kernel(sizes, table, first, rest, own, across, mine, others, turned, near_rows, spread, wide):
    tree = Tree(table, *sizes)
    row, sub = tree.row, tree.sub
    per_two, blocks, rows, cols = own.shape
    for b in range(first.shape[1] // (2 * rows)):
        lanes = slice(b * rows, (b + 1) * rows)
        for out, half in (near_rows, row), (others, 1 - row):
            out[:rows, lanes] = first[:, spot(2 * b + half, rows)]
            out[rows:, lanes] = rest[:, spot(2 * b + half, rows)]
    spread[...] = jnp.zeros_like(spread)
    for h in range(per_two):
        valid, at = tree.level_two(h)
        for t in range(1, blocks):
            span = slice((t - 1) * rows, t * rows)
            spread[spot(at[t - 1], rows), h * cols : (h + 1) * cols] = own[h, t] * valid[t]
            wide[span, spot(sub, cols)] = own[h, t] * valid[t]
            wide[span, spot(1 - sub, cols)] = across[h, t] * valid[t]
        wide[(blocks - 1) * rows :, spot(sub, cols)] = own[h, 0]
        wide[(blocks - 1) * rows :, spot(1 - sub, cols)] = across[h, 0]
        turned[h] = wide[...].T
    mine[...] = mm(near_rows[...], spread[...])


def root_two_kernel(sizes, table, mine, others, turned, beside, lower, inner, spread, tall):
    tree = Tree(table, *sizes)
    per_two, rows, cols = lower.shape[0], lower.shape[2], lower.shape[3]
    blocks = lower.shape[1] + 1
    spread[...] = jnp.zeros_like(spread)
    for h in range(per_two):
        valid, at = tree.level_two(h)
        for t in range(1, blocks):
            spread[spot(at[t - 1], rows), h * cols : (h + 1) * cols] = beside[(blocks * h + t) * rows : (blocks * h + t + 1) * rows] * valid[t]
    total = mine[...] + mm(others[...], spread[...])
    for h in range(per_two):
        for k in range(tree.nodes):
            tall[h, k] = total[k * rows : (k + 1) * rows, h * cols : (h + 1) * cols]
    for h in range(per_two):
        valid, at = tree.level_two(h)
        for t in range(1, blocks):
            lower[h, t - 1] = tall[h, tree.back(at[t - 1])] * valid[t]
        inner[h] = mm(turned[h, :, : (blocks - 1) * rows], lower[h].reshape((blocks - 1) * rows, cols))


def parent_two_kernel(sizes, shifts, table, own, beside, corner, turned, lower, inner, diagonal, *refs):
    tree = Tree(table, *sizes)
    row, sub = tree.row, tree.sub
    blocks, rows, cols = own.shape[1:]
    n = len(shifts)
    panel, diag, sends, cross, top, first, far, part, lead, more = refs[2 * n :]
    low = (blocks - 1) * rows
    for i, k in enumerate(shifts):
        h = tree.child(tree.me, tree.node(-k))
        valid, _ = tree.level_two(h)
        for got, lanes in (refs[2 * i], spot(sub, cols)), (refs[2 * i + 1], spot(1 - sub, cols)):
            cross[:, lanes] = got[:low]
            top[spot(row, rows), lanes] = got[low : low + rows]
            top[spot(1 - row, rows), lanes] = got[low + rows : low + 2 * rows]
        first[spot(row, rows), :] = own[h, 0]
        first[spot(1 - row, rows), :] = beside[h]
        far[:, spot(sub, cols)] = beside[h]
        far[:, spot(1 - sub, cols)] = corner[h]
        below = mm(cross[...], first[...])
        for t in range(1, blocks):
            span = slice((t - 1) * rows, t * rows)
            part[span, :] = below[span, :] * valid[t]
            panel[i, t] = -(lower[h, t - 1] + part[span, :])
        lead[...] = mm(turned[h, spot(sub, cols), :low], cross[...]).T + mm(top[...], first[...])
        mine, other = lead[spot(row, rows), :], lead[spot(1 - row, rows), :]
        part[low:, :] = mine
        more[...] = inner[h] + mm(turned[h], part[...]) + mm_t(far[...], other)
        panel[i, 0] = -mine
        sends[i, 0] = other
        diag[i] = diagonal[h] + more[spot(row, rows), :]
        sends[i, 1] = more[spot(1 - row, rows), :]


def finish_kernel(sizes, groups, table, *refs):
    tree = Tree(table, *sizes)
    n = len(groups)
    panels, diags, gots = refs[:n], refs[n : 2 * n], refs[2 * n : 3 * n]
    keep, got_one, panel_out, diag_out, one_out = refs[3 * n :]
    one_out[...] = keep[...] + got_one[...]
    for j, shifts in enumerate(groups):
        for i, k in enumerate(shifts):
            h = tree.child(tree.me, tree.node(-k))
            panel_out[h, 1:] = panels[j][i, 1:]
            panel_out[h, 0] = panels[j][i, 0] - gots[j][i, 0]
            diag_out[h] = diags[j][i] + gots[j][i, 1]


def shift(x, axis, k):
    n = lax.axis_size(axis)
    return lax.ppermute(x, axis, [(i, (i + k) % n) for i in range(n)])


def after(x, *others):
    return lax.optimization_barrier((x,) + others)[0]


def paired_shards(root_inverse, panel_one, diag_one, panel_two, diag_two, ancestors, counts, owners, slots, offsets):
    nodes = lax.axis_size("node")
    me, row, sub = lax.axis_index("node"), lax.axis_index("row"), lax.axis_index("sub")
    per_one, blocks, rows, cols = panel_one.shape
    per_two = panel_two.shape[0]
    sizes = nodes, per_one, per_two
    full = root_inverse.shape[2] * root_inverse.shape[3]
    low = (blocks - 1) * rows
    table = jnp.concatenate(
        [jnp.stack([me, row, sub]).astype(jnp.int32), counts, owners, slots, ancestors.T.reshape(-1), offsets.T.reshape(-1)]
    )
    bind = lambda kernel, *more: functools.partial(kernel, sizes, *more)
    together = lax.optimization_barrier

    half = lax.dynamic_slice_in_dim(root_inverse[0], sub * (rows // 2), rows // 2, 0)
    half = half.reshape(rows // 2, full // cols, cols).transpose(1, 0, 2).reshape(-1, cols)
    half = jnp.pad(half, ((0, 8), (0, 0)))
    far = [shift(half, "node", k) for k in range(1, nodes)]
    source = after(panel_one, table)
    beside_one = [shift(source[g : g + 1], "row", 1) for g in range(per_one)]
    first, spread, total = call(
        bind(early_kernel),
        [array(rows, full), array(full, per_one * cols), array(rows, per_one * cols)],
        table,
        [root_inverse[0], panel_one, *beside_one],
    )
    *far, total = together((*far, total))
    near = [shift(x, "sub", 1) for x in far]
    across_one = shift(after(panel_one, far[0]), "sub", 1)
    flat = jnp.pad(panel_two.reshape(per_two * blocks * rows, cols), ((0, 16), (0, 0)))
    beside_two = shift(after(flat, far[0]), "row", 1)

    rest, cov_panel_one, keep, send, *parents = call(
        bind(level_one_kernel),
        [array((nodes - 1) * rows, full), array(*panel_one.shape), array(per_one, rows, cols), array(per_one, rows, cols)]
        + [array((blocks + 1) * rows + SPARE.get(k, 0), cols) for k in range(nodes)],
        table,
        [spread, total, panel_one, across_one, diag_one] + far + near,
        [(blocks * rows, 2 * cols), (per_one, nodes, rows, cols), (2 * rows, cols)],
    )
    parents = [x if k == 0 else shift(x, "node", k) for k, x in enumerate(parents)]
    got_one = shift(send, "row", 1)
    across_two = shift(after(panel_two, send), "sub", 1)

    own_part, others, turned = call(
        bind(prepare_two_kernel),
        [array(nodes * rows, per_two * cols), array(nodes * rows, full // 2), array(per_two, 2 * rows, low + rows)],
        table,
        [first, rest, panel_two, across_two],
        [(nodes * rows, full // 2), (full // 2, per_two * cols), (low + rows, 2 * cols)],
    )
    beside_two, own_part = together((beside_two, own_part))
    (first_beside,) = plain(first_blocks_kernel, [array(per_two, rows, cols)], beside_two)
    corner_two = shift(first_beside, "sub", 1)
    lower, inner = call(
        bind(root_two_kernel),
        [array(per_two, blocks - 1, rows, cols), array(per_two, 2 * rows, cols)],
        table,
        [own_part, others, turned, beside_two],
        [(full // 2, per_two * cols), (per_two, nodes, rows, cols)],
    )
    panels, diags, gots, sent = [], [], [], []
    for k in ORDER:
        mine = parents[k]
        if k == ORDER[1]:
            mine = after(mine, lower)
        if k in ORDER[2:]:
            mine = after(mine, *sent[:2])
        side = shift(mine, "sub", 1)
        if k == ORDER[1]:
            mine = after(mine, got_one)
        panel, diag, sends = call(
            bind(parent_two_kernel, (k,)),
            [array(1, blocks, rows, cols), array(1, rows, cols), array(1, 2, rows, cols)],
            table,
            [panel_two, first_beside, corner_two, turned, lower, inner, diag_two, mine, side],
            [
                (low, 2 * cols),
                (2 * rows, 2 * cols),
                (2 * rows, cols),
                (rows, 2 * cols),
                (low + rows, cols),
                (2 * rows, cols),
                (2 * rows, cols),
            ],
        )
        sent.append(sends)
        panels.append(panel)
        diags.append(diag)
        gots.append(shift(sends, "row", 1))
    cov_panel_two, cov_diag_two, cov_diag_one = call(
        bind(finish_kernel, tuple((k,) for k in ORDER)),
        [array(*panel_two.shape), array(*diag_two.shape), array(*diag_one.shape)],
        table,
        panels + diags + gots + [keep, got_one],
    )
    return (cov_panel_one, cov_diag_one, cov_panel_two, cov_diag_two)


def pick_blocks(gathered, block_ids):
    return gathered[block_ids[:, :, None], :, block_ids[:, None, :]]


def apply_panel(matrix, masked):
    return jnp.einsum(
        "kabic,kbcj->kaij",
        matrix,
        lax.all_gather(masked, "row", axis=2, tiled=True),
        precision=PRECISE,
    )


def diag_update(masked, column, diagonal):
    full_cols = lax.all_gather(masked, "sub", axis=3, tiled=True)
    summed = lax.psum_scatter(
        jnp.einsum("kaij,kail->jkl", full_cols, column, precision=PRECISE),
        "row",
        scatter_dimension=0,
        tiled=True,
    )
    return diagonal - jnp.transpose(summed, (1, 0, 2))


def general_shards(
    root_inverse,
    panel_one,
    diag_one,
    panel_two,
    diag_two,
    ancestors,
    counts,
    owners,
    slots,
    offsets,
):
    nodes = lax.axis_size("node")
    own_index = lax.axis_index("node")
    per_one = panel_one.shape[0]
    per_two = panel_two.shape[0]
    rows_here = panel_one.shape[2]
    width = root_inverse.shape[3]
    positions = jnp.arange(A, dtype=jnp.int32)
    my_ids = lax.dynamic_slice_in_dim(ancestors, own_index * per_one, per_one, 0)
    my_counts = lax.dynamic_slice_in_dim(counts, own_index * per_one, per_one, 0)
    valid_one = (positions[None, :] < my_counts[:, None]).astype(jnp.float32)
    my_owner = lax.dynamic_slice_in_dim(owners, own_index * per_two, per_two, 0)
    my_slot = lax.dynamic_slice_in_dim(slots, own_index * per_two, per_two, 0)
    my_offsets = lax.dynamic_slice_in_dim(offsets, own_index * per_two, per_two, 0)
    my_parent = my_owner * per_one + my_slot
    parent_count = jnp.take(counts, my_parent)
    valid_two = (positions[None, :] < jnp.minimum(A, 1 + parent_count)[:, None]).astype(jnp.float32)
    gathered = lax.all_gather(root_inverse, "node", axis=0, tiled=True)
    block_one = pick_blocks(gathered, my_ids)
    parent_ids = jnp.take_along_axis(jnp.take(ancestors, my_parent, axis=0), my_offsets, axis=1)
    separator = pick_blocks(gathered, parent_ids)
    block_one = block_one * valid_one[:, :, None, None, None]
    masked_one = panel_one * valid_one[:, :, None, None]
    cov_panel_one = -apply_panel(block_one, masked_one)
    cov_diag_one = diag_update(masked_one, cov_panel_one, diag_one)
    full_cross, full_diag = (
        lax.all_gather(cov_panel_one, "sub", axis=3, tiled=True),
        lax.all_gather(cov_diag_one, "sub", axis=2, tiled=True),
    )
    owner_grid = owners.reshape(nodes, per_two)
    child_match = (owner_grid == own_index).astype(jnp.int32)
    has_child = jnp.sum(child_match, axis=1)
    child_pos = jnp.sum(child_match * jnp.arange(per_two, dtype=jnp.int32)[None, :], axis=1)
    child_index = jnp.arange(nodes, dtype=jnp.int32) * per_two + child_pos
    parent_slot = jnp.take(slots, child_index)
    parent_pos = jnp.take(offsets, child_index, axis=0)
    present = has_child.astype(jnp.float32)
    top_send = jnp.take(full_diag, parent_slot, axis=0) * present[:, None, None]
    cross_pick = jnp.take(
        full_cross.reshape(per_one * A, rows_here, width),
        parent_slot[:, None] * A + parent_pos,
        axis=0,
    )
    cross_pick = cross_pick * present[:, None, None, None]
    got_top, got_cross = (
        lax.all_to_all(top_send, "node", split_axis=0, concat_axis=0, tiled=True),
        lax.all_to_all(cross_pick, "node", split_axis=0, concat_axis=0, tiled=True),
    )
    my_cross = jnp.take(got_cross, my_owner, axis=0)
    my_lower = jnp.concatenate([my_cross[:, :, None], separator], axis=2)
    my_top = jnp.take(got_top, my_owner, axis=0)
    empty_blocks = jnp.zeros((per_two, 1, A - 1, rows_here, width), jnp.float32)
    first_row = jnp.concatenate([my_top[:, None, None], empty_blocks], axis=2)
    block_two = jnp.concatenate([first_row, my_lower], axis=1) * valid_two[:, :, None, None, None]
    masked_two = panel_two * valid_two[:, :, None, None]
    lower_part = apply_panel(block_two, masked_two)
    beside = my_lower[:, :, 0]
    further = masked_two[:, 1:]
    upper_part = lax.psum_scatter(
        jnp.einsum("ktci,ktcj->ikj", beside, further, precision=PRECISE),
        "row",
        scatter_dimension=0,
        tiled=True,
    )
    first_block = lower_part[:, 0] + jnp.transpose(upper_part, (1, 0, 2))
    cov_panel_two = -jnp.concatenate([first_block[:, None], lower_part[:, 1:]], axis=1)
    cov_diag_two = diag_update(masked_two, cov_panel_two, diag_two)
    return (cov_panel_one, cov_diag_one, cov_panel_two, cov_diag_two)


def shards(*args):
    sizes = lax.axis_size("node"), lax.axis_size("row"), lax.axis_size("sub")
    root, panel_one, panel_two = args[0], args[1], args[3]
    if sizes == (4, 2, 2) and panel_two.shape[0] == root.shape[2] == panel_one.shape[1] == A and root.shape[0] == 1:
        return paired_shards(*args)
    return general_shards(*args)


def solution(mesh):
    return jax.shard_map(
        shards,
        mesh=mesh,
        in_specs=(
            P(("groups", "node"), "row", None, None),
            P(("groups", "node"), None, "row", "sub"),
            P(("groups", "node"), "row", "sub"),
            P(("groups", "node"), None, "row", "sub"),
            P(("groups", "node"), "row", "sub"),
            P("groups", None),
            P("groups"),
            P("groups"),
            P("groups"),
            P("groups", None),
        ),
        out_specs=(
            P(("groups", "node"), None, "row", "sub"),
            P(("groups", "node"), "row", "sub"),
            P(("groups", "node"), None, "row", "sub"),
            P(("groups", "node"), "row", "sub"),
        ),
        check_vma=False,
    )
```
